32 devices in a mesh: mem: 2 (over core), lat: 16 (over z, y, x).
Axes of the slice: x: 2, y: 2, z: 4, core: 2. Of those that a mesh axis runs over, the one named last changes fastest.
Arguments:
- perturbations: bfloat16 [32, 2, 4, 64, 1440], P('mem', None, None, 'lat'), may hold values from -1 to 1
- gradient_held: float32 [2, 4, 64, 1440], P(None, 'mem', 'lat'), may hold values from -6 to 6
- block_owner: int32 [4], replicated, may hold values from 0 to 3, each once
Outputs:
- increment_held: float32 [2, 4, 64, 1440], P(None, 'mem', 'lat')
The draws below stay inside these ranges and needn't reach their ends.
Inputs may be any that keep to these rules, and one draw needn't show every extreme that they name: `block_owner`: each value appears exactly once.
All inputs are finite; a program needn't handle non-finite values.
Results may differ from the reference program's by a relative error of at most 0.0022.
Values may be sent and summed in bfloat16 or wider, within the bound.
A program may use at most 128 MiB of HBM per device.

```python
import math
import jax
import jax.numpy as jnp
from jax import lax

LON = 1440
SLOTS = 2
MEMBERS = 32
LEV = 4
LAT = 64


def draw_perturbations(key, part):
    subkeys = jax.random.split(key, 1)
    full_shape = (MEMBERS, SLOTS, LEV, LAT, LON)
    spread = 1.0 / math.sqrt(MEMBERS)
    white_noise = jax.random.normal(subkeys[0], full_shape, jnp.float32)
    values = spread * white_noise
    return jnp.clip(values, -1.0, 1.0).astype(jnp.bfloat16)


def draw_gradient_held(key, part):
    subkeys = jax.random.split(key, 1)
    full_shape = (SLOTS, LEV, LAT, LON)
    white_noise = jax.random.normal(subkeys[0], full_shape, jnp.float32)
    values = white_noise
    return jnp.clip(values, -6.0, 6.0).astype(jnp.float32)


def setup_inputs(seed: int = 0) -> dict:
    streams_of = jax.random.split(jax.random.key(seed), 4)
    perturbations = draw_perturbations(jax.random.fold_in(streams_of[3], 71), 0)
    gradient_held = draw_gradient_held(jax.random.fold_in(streams_of[3], 71), 0)
    block_owner = jax.random.permutation(streams_of[2], LEV).astype(jnp.int32)
    return dict(perturbations=perturbations, gradient_held=gradient_held, block_owner=block_owner)


def weights_for(spread_cells):
    return [math.exp(-(offset * offset) / (2.0 * spread_cells * spread_cells)) for offset in range(-4, 5)]


def smooth_periodic(source, along_dim, weights):
    summed = jnp.zeros_like(source)
    for offset in range(-4, 5):
        summed = summed + weights[offset + 4] * jnp.roll(source, -offset, axis=along_dim)
    return summed


def smooth_bounded(source, along_dim, weights):
    length = source.shape[along_dim]
    widths = [(0, 0)] * source.ndim
    widths[along_dim] = (4, 4)
    padded = jnp.pad(source, widths)
    summed = jnp.zeros_like(source)
    for offset in range(-4, 5):
        summed = summed + weights[offset + 4] * lax.slice_in_dim(padded, 4 + offset, 4 + offset + length, axis=along_dim)
    return summed


def reference(perturbations, gradient_held, block_owner):
    places = jnp.arange(LEV, dtype=jnp.int32)
    owners = block_owner.astype(jnp.int32)
    inverse = jnp.sum(jnp.where(owners[None, :] == places[:, None], places[None, :], 0), axis=1).astype(jnp.int32)
    gradient = jnp.take(gradient_held, inverse, axis=1)
    lon_weights = weights_for(3.0)
    lev_weights = weights_for(2.0)
    lat_weights = weights_for(2.5)

    def member_step(summed, member):
        widened = member.astype(jnp.float32)
        control = jnp.sum(widened * gradient, axis=0).astype(jnp.bfloat16)
        control = lax.optimization_barrier(control).astype(jnp.float32)
        smoothed = smooth_periodic(control, 2, lon_weights)
        smoothed = smooth_bounded(smoothed, 0, lev_weights)
        smoothed = smooth_bounded(smoothed, 1, lat_weights)
        return summed + widened * smoothed[None], None

    start = jnp.zeros((SLOTS, LEV, LAT, LON), jnp.float32)
    increment, unused = lax.scan(member_step, start, perturbations)
    return jnp.take(increment, owners, axis=1)
```

```python
import functools
import math

import jax
import jax.numpy as jnp
import ml_dtypes
import numpy as np
from jax import lax
from jax.experimental import pallas as pl
from jax.experimental.pallas import tpu as pltpu
from jax.sharding import PartitionSpec as P

MESH = pl.DeviceIdType.MESH
REACH = 4
EDGE = 128
TILE = 256
F32 = jnp.float32
BF16 = jnp.bfloat16


def rho(offset, spread):
    if abs(offset) > REACH:
        return 0.0
    return math.exp(-(offset * offset) / (2.0 * spread * spread))


def split_weights(exact):
    high = exact.astype(ml_dtypes.bfloat16)
    low = (exact - high.astype(np.float64)).astype(ml_dtypes.bfloat16)
    return high, low


def level_row_weights(levels, rows, group):
    lev = np.array([[rho(a - b, 2.0) for b in range(levels)] for a in range(levels)])

    def block(shift):
        lat = np.array([[rho(b + shift * rows - a, 2.5) for b in range(rows)] for a in range(rows)])
        return np.kron(np.eye(group), np.kron(lev, lat))

    both = []
    for direct in (1, -1):
        high, low = split_weights(np.concatenate([block(0), block(direct), block(-direct)], axis=1))
        both.append(np.concatenate([high, low], axis=0))
    return np.stack(both)


def fill_lon_weights(wlon):
    shape = wlon.shape[1:]
    inward = lax.broadcasted_iota(jnp.int32, shape, 0)
    outward = lax.broadcasted_iota(jnp.int32, shape, 1)
    apart = jnp.abs(inward - EDGE - outward)
    halves = split_weights(np.array([rho(a, 3.0) for a in range(REACH + 1)]))
    for half in range(2):
        band = jnp.zeros(shape, F32)
        for a in range(REACH + 1):
            band = jnp.where(apart == a, float(halves[half][a]), band)
        wlon[half] = band.astype(BF16)


def kernel(
    group, owner, pert, held, wlat, out,
    wlon, gbuf, gord, cbuf, dbuf, rbuf, total, levelled, give, take,
    g_send, g_recv, c_send, c_recv, f_send, f_recv, t_send, t_recv,
):
    members, slots, depth, lon = pert.shape
    holders, _, held_levels, rows, _ = gbuf.shape
    levels = depth // rows
    chunks = members // group
    tiles = -(-lon // TILE)
    right_pad = tiles * TILE + EDGE - lon

    me = lax.axis_index("mem")
    here = lax.axis_index("lat")
    count = lax.axis_size("lat")
    parity = lax.rem(here, 2)
    partner = here + 1 - 2 * parity
    hop = 2 - 4 * parity
    target = here + hop
    source = here - hop
    has_target = jnp.logical_and(target >= 0, target < count)
    has_source = jnp.logical_and(source >= 0, source < count)

    barrier = pltpu.get_barrier_semaphore()
    for k in range(1, holders):
        pl.semaphore_signal(
            barrier, inc=1, device_id=(lax.rem(me + k, holders), here), device_id_type=MESH
        )
    pl.semaphore_signal(barrier, inc=1, device_id=(me, partner), device_id_type=MESH)

    @pl.when(has_target)
    def _():
        pl.semaphore_signal(barrier, inc=1, device_id=(me, target), device_id_type=MESH)

    @pl.when(has_source)
    def _():
        pl.semaphore_signal(barrier, inc=1, device_id=(me, source), device_id_type=MESH)

    pl.semaphore_wait(barrier, holders + has_target.astype(jnp.int32) + has_source.astype(jnp.int32))

    def gradient_copy(k):
        return pltpu.make_async_remote_copy(
            src_ref=held, dst_ref=gbuf.at[me],
            send_sem=g_send.at[k - 1], recv_sem=g_recv.at[k - 1],
            device_id=(lax.rem(me + k, holders), here), device_id_type=MESH,
        )

    for k in range(1, holders):
        gradient_copy(k).start()
    gbuf[me] = held[...]
    fill_lon_weights(wlon)

    @pl.when(jnp.logical_not(has_source))
    def _():
        rbuf[...] = jnp.zeros_like(rbuf)

    total[...] = jnp.zeros_like(total)
    for k in range(1, holders):
        gradient_copy(k).wait()

    for level in range(levels):
        place = jnp.int32(0)
        for p in range(levels):
            place = jnp.where(owner[p] == level, p, place)
        holder = lax.div(place, held_levels)
        within = lax.rem(place, held_levels)
        for slot in range(slots):
            gord[slot, level * rows:(level + 1) * rows, :] = gbuf[holder, slot, within]

    def own_copy(c):
        span = pl.ds(c * group, group)
        return pltpu.make_async_remote_copy(
            src_ref=cbuf.at[span], dst_ref=dbuf.at[span],
            send_sem=c_send.at[c], recv_sem=c_recv.at[c],
            device_id=(me, partner), device_id_type=MESH,
        )

    def relay_copy(c):
        span = pl.ds(c * group, group)
        return pltpu.make_async_remote_copy(
            src_ref=dbuf.at[span], dst_ref=rbuf.at[span],
            send_sem=f_send.at[c], recv_sem=f_recv.at[c],
            device_id=(me, target), device_id_type=MESH,
        )

    def control_step(c, carry):
        for i in range(group):
            m = c * group + i
            value = pert[m, 0].astype(F32) * gord[0]
            for slot in range(1, slots):
                value = value + pert[m, slot].astype(F32) * gord[slot]
            cbuf[m] = value.astype(BF16)
        own_copy(c).start()
        return carry

    lax.fori_loop(0, chunks, control_step, 0)

    def relay(c):
        own_copy(c).wait_recv()

        @pl.when(has_target)
        def _():
            relay_copy(c).start()

    def process(c):
        @pl.when(has_source)
        def _():
            relay_copy(c).wait_recv()

        span = pl.ds(c * group, group)
        block = group * depth
        stack = jnp.concatenate(
            [buf[span].reshape(block, lon) for buf in (cbuf, dbuf, rbuf)], axis=0
        )
        mixed = jnp.dot(wlat[parity], stack, preferred_element_type=F32)
        mixed = mixed[:block] + mixed[block:]
        ringed = jnp.concatenate(
            [mixed[:, lon - EDGE:], mixed, mixed[:, :right_pad]], axis=1
        )
        high = ringed.astype(BF16)
        low = (ringed - high.astype(F32)).astype(BF16)
        width = TILE + 2 * EDGE
        highs = [high[:, t * TILE:t * TILE + width] for t in range(tiles)]
        lows = [low[:, t * TILE:t * TILE + width] for t in range(tiles)]
        first = jnp.dot(
            jnp.concatenate(highs + lows, axis=0), wlon[0], preferred_element_type=F32
        )
        second = jnp.dot(jnp.concatenate(highs, axis=0), wlon[1], preferred_element_type=F32)
        smoothed = first[:tiles * block] + first[tiles * block:] + second
        for t in range(tiles):
            low_lon, high_lon = t * TILE, min((t + 1) * TILE, lon)
            for slot in range(slots):
                summed = total[slot, :, low_lon:high_lon]
                for i in range(group):
                    part = smoothed[t * block + i * depth:t * block + (i + 1) * depth]
                    summed = summed + (
                        pert[c * group + i, slot, :, low_lon:high_lon].astype(F32)
                        * part[:, :high_lon - low_lon]
                    )
                total[slot, :, low_lon:high_lon] = summed

    relay(0)

    def step(c, carry):
        relay(c + 1)
        process(c)
        return carry

    lax.fori_loop(0, chunks - 1, step, 0)
    process(chunks - 1)

    for level in range(levels):
        for slot in range(slots):
            levelled[slot, level] = total[slot, level * rows:(level + 1) * rows, :]

    def total_copy(k):
        return pltpu.make_async_remote_copy(
            src_ref=give.at[k - 1], dst_ref=take.at[k - 1],
            send_sem=t_send.at[k - 1], recv_sem=t_recv.at[k - 1],
            device_id=(lax.rem(me + k, holders), here), device_id_type=MESH,
        )

    for k in range(1, holders):
        holder = lax.rem(me + k, holders)
        for r in range(held_levels):
            level = owner[holder * held_levels + r]
            for slot in range(slots):
                give[k - 1, slot, r] = levelled[slot, level]
        total_copy(k).start()

    def drain(c, carry):
        own_copy(c).wait_send()

        @pl.when(has_target)
        def _():
            relay_copy(c).wait_send()

        return carry

    lax.fori_loop(0, chunks, drain, 0)
    for k in range(1, holders):
        total_copy(k).wait()
    for r in range(held_levels):
        level = owner[me * held_levels + r]
        for slot in range(slots):
            value = levelled[slot, level]
            for k in range(1, holders):
                value = value + take[k - 1, slot, r]
            out[slot, r] = value


def local(group, perturbations, gradient_held, block_owner):
    members, slots, levels, rows, lon = perturbations.shape
    held_levels = gradient_held.shape[1]
    holders = lax.axis_size("mem")
    depth = levels * rows
    chunks = members // group
    others = max(holders - 1, 1)
    wlat = jnp.asarray(level_row_weights(levels, rows, group))
    vmem = pl.BlockSpec(memory_space=pltpu.VMEM)
    part = (slots, held_levels, rows, lon)
    dma = pltpu.SemaphoreType.DMA
    return pl.pallas_call(
        functools.partial(kernel, group),
        out_shape=jax.ShapeDtypeStruct(part, F32),
        in_specs=[pl.BlockSpec(memory_space=pltpu.SMEM)] + [vmem] * 3,
        out_specs=vmem,
        scratch_shapes=[
            pltpu.VMEM((2, TILE + 2 * EDGE, TILE), BF16),
            pltpu.VMEM((holders,) + part, F32),
            pltpu.VMEM((slots, depth, lon), F32),
            pltpu.VMEM((members, depth, lon), BF16),
            pltpu.VMEM((members, depth, lon), BF16),
            pltpu.VMEM((members, depth, lon), BF16),
            pltpu.VMEM((slots, depth, lon), F32),
            pltpu.VMEM((slots, levels, rows, lon), F32),
            pltpu.VMEM((others,) + part, F32),
            pltpu.VMEM((others,) + part, F32),
            dma((others,)), dma((others,)),
            dma((chunks,)), dma((chunks,)),
            dma((chunks,)), dma((chunks,)),
            dma((others,)), dma((others,)),
        ],
        compiler_params=pltpu.CompilerParams(
            collective_id=0, has_side_effects=True, vmem_limit_bytes=48 * 1024 * 1024
        ),
    )(
        block_owner,
        perturbations.reshape(members, slots, depth, lon),
        gradient_held, wlat,
    )


def solution(mesh):
    placed = (P("mem", None, None, "lat", None), P(None, "mem", "lat", None), P())
    return jax.shard_map(
        functools.partial(local, 2),
        mesh=mesh, in_specs=placed, out_specs=P(None, "mem", "lat", None), check_vma=False,
    )
```

```python
import functools
import math

import jax
import jax.numpy as jnp
import ml_dtypes
import numpy as np
from jax import lax
from jax.experimental import pallas as pl
from jax.experimental.pallas import tpu as pltpu
from jax.sharding import PartitionSpec as P

MESH = pl.DeviceIdType.MESH
REACH = 4
EDGE = 128
TILE = 256
F32 = jnp.float32
BF16 = jnp.bfloat16


def rho(offset, spread):
    if abs(offset) > REACH:
        return 0.0
    return math.exp(-(offset * offset) / (2.0 * spread * spread))


def split_weights(exact):
    high = exact.astype(ml_dtypes.bfloat16)
    low = (exact - high.astype(np.float64)).astype(ml_dtypes.bfloat16)
    return high, low


def level_row_weights(levels, rows, group):
    lev = np.array([[rho(a - b, 2.0) for b in range(levels)] for a in range(levels)])

    def block(shift):
        lat = np.array([[rho(b + shift * rows - a, 2.5) for b in range(rows)] for a in range(rows)])
        return np.kron(np.eye(group), np.kron(lev, lat))

    both = []
    for direct in (1, -1):
        high, low = split_weights(np.concatenate([block(0), block(direct), block(-direct)], axis=1))
        both.append(np.concatenate([high, low], axis=0))
    return np.stack(both)


def fill_lon_weights(wlon):
    shape = wlon.shape[1:]
    inward = lax.broadcasted_iota(jnp.int32, shape, 0)
    outward = lax.broadcasted_iota(jnp.int32, shape, 1)
    apart = jnp.abs(inward - EDGE - outward)
    halves = split_weights(np.array([rho(a, 3.0) for a in range(REACH + 1)]))
    for half in range(2):
        band = jnp.zeros(shape, F32)
        for a in range(REACH + 1):
            band = jnp.where(apart == a, float(halves[half][a]), band)
        wlon[half] = band.astype(BF16)


def kernel(
    group, ahead, owner, fields, held, wlat, out,
    raw, pert, wlon, gbuf, gord, cbuf, dbuf, rbuf, total, levelled, give, take,
    p_sem, g_send, g_recv, c_send, c_recv, f_send, f_recv, t_send, t_recv,
):
    members, slots, depth, lon = pert.shape
    holders, _, held_levels, rows, _ = gbuf.shape
    levels = depth // rows
    chunks = members // group
    tiles = -(-lon // TILE)
    right_pad = tiles * TILE + EDGE - lon

    def field_copy(m):
        return pltpu.make_async_copy(fields.at[m], raw.at[m], p_sem.at[m])

    def start_fields(m, carry):
        field_copy(m).start()
        return carry

    lax.fori_loop(0, members, start_fields, 0)

    me = lax.axis_index("mem")
    here = lax.axis_index("lat")
    count = lax.axis_size("lat")
    parity = lax.rem(here, 2)
    partner = here + 1 - 2 * parity
    hop = 2 - 4 * parity
    target = here + hop
    source = here - hop
    has_target = jnp.logical_and(target >= 0, target < count)
    has_source = jnp.logical_and(source >= 0, source < count)

    barrier = pltpu.get_barrier_semaphore()
    for k in range(1, holders):
        pl.semaphore_signal(
            barrier, inc=1, device_id=(lax.rem(me + k, holders), here), device_id_type=MESH
        )
    pl.semaphore_signal(barrier, inc=1, device_id=(me, partner), device_id_type=MESH)

    @pl.when(has_target)
    def _():
        pl.semaphore_signal(barrier, inc=1, device_id=(me, target), device_id_type=MESH)

    @pl.when(has_source)
    def _():
        pl.semaphore_signal(barrier, inc=1, device_id=(me, source), device_id_type=MESH)

    fill_lon_weights(wlon)

    @pl.when(jnp.logical_not(has_source))
    def _():
        rbuf[...] = jnp.zeros_like(rbuf)

    pl.semaphore_wait(barrier, holders + has_target.astype(jnp.int32) + has_source.astype(jnp.int32))

    def gradient_copy(k):
        return pltpu.make_async_remote_copy(
            src_ref=held, dst_ref=gbuf.at[me],
            send_sem=g_send.at[k - 1], recv_sem=g_recv.at[k - 1],
            device_id=(lax.rem(me + k, holders), here), device_id_type=MESH,
        )

    for k in range(1, holders):
        gradient_copy(k).start()
    gbuf[me] = held[...]
    total[...] = jnp.zeros_like(total)
    for k in range(1, holders):
        gradient_copy(k).wait()

    for level in range(levels):
        place = jnp.int32(0)
        for p in range(levels):
            place = jnp.where(owner[p] == level, p, place)
        holder = lax.div(place, held_levels)
        within = lax.rem(place, held_levels)
        for slot in range(slots):
            gord[slot, level * rows:(level + 1) * rows, :] = gbuf[holder, slot, within]

    def own_copy(c):
        span = pl.ds(c * group, group)
        return pltpu.make_async_remote_copy(
            src_ref=cbuf.at[span], dst_ref=dbuf.at[span],
            send_sem=c_send.at[c], recv_sem=c_recv.at[c],
            device_id=(me, partner), device_id_type=MESH,
        )

    def relay_copy(c):
        span = pl.ds(c * group, group)
        return pltpu.make_async_remote_copy(
            src_ref=dbuf.at[span], dst_ref=rbuf.at[span],
            send_sem=f_send.at[c], recv_sem=f_recv.at[c],
            device_id=(me, target), device_id_type=MESH,
        )

    def control_step(c, carry):
        for i in range(group):
            m = c * group + i
            field_copy(m).wait()
            value = None
            for slot in range(slots):
                field = jnp.concatenate(
                    [raw[m, slot, level].astype(F32) for level in range(levels)], axis=0
                )
                pert[m, slot] = field.astype(BF16)
                term = field * gord[slot]
                value = term if value is None else value + term
            cbuf[m] = value.astype(BF16)
        own_copy(c).start()
        return carry

    lax.fori_loop(0, chunks, control_step, 0)

    def relay(c):
        own_copy(c).wait_recv()

        @pl.when(has_target)
        def _():
            relay_copy(c).start()

    def process(c):
        @pl.when(has_source)
        def _():
            relay_copy(c).wait_recv()

        span = pl.ds(c * group, group)
        block = group * depth
        stack = jnp.concatenate(
            [buf[span].reshape(block, lon) for buf in (cbuf, dbuf, rbuf)], axis=0
        )
        mixed = jnp.dot(wlat[parity], stack, preferred_element_type=F32)
        mixed = mixed[:block] + mixed[block:]
        ringed = jnp.concatenate(
            [mixed[:, lon - EDGE:], mixed, mixed[:, :right_pad]], axis=1
        )
        high = ringed.astype(BF16)
        low = (ringed - high.astype(F32)).astype(BF16)
        width = TILE + 2 * EDGE
        highs = [high[:, t * TILE:t * TILE + width] for t in range(tiles)]
        lows = [low[:, t * TILE:t * TILE + width] for t in range(tiles)]
        first = jnp.dot(
            jnp.concatenate(highs + lows, axis=0), wlon[0], preferred_element_type=F32
        )
        second = jnp.dot(jnp.concatenate(highs, axis=0), wlon[1], preferred_element_type=F32)
        smoothed = first[:tiles * block] + first[tiles * block:] + second
        for t in range(tiles):
            low_lon, high_lon = t * TILE, min((t + 1) * TILE, lon)
            for slot in range(slots):
                summed = total[slot, :, low_lon:high_lon]
                for i in range(group):
                    part = smoothed[t * block + i * depth:t * block + (i + 1) * depth]
                    summed = summed + (
                        pert[c * group + i, slot, :, low_lon:high_lon].astype(F32)
                        * part[:, :high_lon - low_lon]
                    )
                total[slot, :, low_lon:high_lon] = summed

    lead = min(ahead, chunks)

    def relay_step(c, carry):
        relay(c)
        return carry

    def step(c, carry):
        relay(c + lead)
        process(c)
        return carry

    def last_step(c, carry):
        process(c)
        return carry

    lax.fori_loop(0, lead, relay_step, 0)
    lax.fori_loop(0, chunks - lead, step, 0)
    lax.fori_loop(chunks - lead, chunks, last_step, 0)

    for level in range(levels):
        for slot in range(slots):
            levelled[slot, level] = total[slot, level * rows:(level + 1) * rows, :]

    def total_copy(k):
        return pltpu.make_async_remote_copy(
            src_ref=give.at[k - 1], dst_ref=take.at[k - 1],
            send_sem=t_send.at[k - 1], recv_sem=t_recv.at[k - 1],
            device_id=(lax.rem(me + k, holders), here), device_id_type=MESH,
        )

    for k in range(1, holders):
        holder = lax.rem(me + k, holders)
        for r in range(held_levels):
            level = owner[holder * held_levels + r]
            for slot in range(slots):
                give[k - 1, slot, r] = levelled[slot, level]
        total_copy(k).start()

    def drain(c, carry):
        own_copy(c).wait_send()

        @pl.when(has_target)
        def _():
            relay_copy(c).wait_send()

        return carry

    lax.fori_loop(0, chunks, drain, 0)
    for k in range(1, holders):
        total_copy(k).wait()
    for r in range(held_levels):
        level = owner[me * held_levels + r]
        for slot in range(slots):
            value = levelled[slot, level]
            for k in range(1, holders):
                value = value + take[k - 1, slot, r]
            out[slot, r] = value


def local(group, ahead, perturbations, gradient_held, block_owner):
    members, slots, levels, rows, lon = perturbations.shape
    held_levels = gradient_held.shape[1]
    holders = lax.axis_size("mem")
    depth = levels * rows
    chunks = members // group
    others = max(holders - 1, 1)
    wlat = jnp.asarray(level_row_weights(levels, rows, group))
    vmem = pl.BlockSpec(memory_space=pltpu.VMEM)
    part = (slots, held_levels, rows, lon)
    dma = pltpu.SemaphoreType.DMA
    return pl.pallas_call(
        functools.partial(kernel, group, ahead),
        out_shape=jax.ShapeDtypeStruct(part, F32),
        in_specs=[
            pl.BlockSpec(memory_space=pltpu.SMEM), pl.BlockSpec(memory_space=pltpu.HBM), vmem, vmem,
        ],
        out_specs=vmem,
        scratch_shapes=[
            pltpu.VMEM((members, slots, levels, rows, lon), BF16),
            pltpu.VMEM((members, slots, depth, lon), BF16),
            pltpu.VMEM((2, TILE + 2 * EDGE, TILE), BF16),
            pltpu.VMEM((holders,) + part, F32),
            pltpu.VMEM((slots, depth, lon), F32),
            pltpu.VMEM((members, depth, lon), BF16),
            pltpu.VMEM((members, depth, lon), BF16),
            pltpu.VMEM((members, depth, lon), BF16),
            pltpu.VMEM((slots, depth, lon), F32),
            pltpu.VMEM((slots, levels, rows, lon), F32),
            pltpu.VMEM((others,) + part, F32),
            pltpu.VMEM((others,) + part, F32),
            dma((members,)),
            dma((others,)), dma((others,)),
            dma((chunks,)), dma((chunks,)),
            dma((chunks,)), dma((chunks,)),
            dma((others,)), dma((others,)),
        ],
        compiler_params=pltpu.CompilerParams(
            collective_id=0, has_side_effects=True, vmem_limit_bytes=63 * 1024 * 1024
        ),
    )(
        block_owner, perturbations, gradient_held, wlat,
    )


def solution(mesh):
    placed = (P("mem", None, None, "lat", None), P(None, "mem", "lat", None), P())
    return jax.shard_map(
        functools.partial(local, 1, 3),
        mesh=mesh, in_specs=placed, out_specs=P(None, "mem", "lat", None), check_vma=False,
    )
```

```python
import functools
import math

import jax
import jax.numpy as jnp
import ml_dtypes
import numpy as np
from jax import lax
from jax.experimental import pallas as pl
from jax.experimental.pallas import tpu as pltpu
from jax.sharding import PartitionSpec as P

MESH = pl.DeviceIdType.MESH
REACH = 4
LANES = 128
F32 = jnp.float32
BF16 = jnp.bfloat16


def rho(offset, spread):
    if abs(offset) > REACH:
        return 0.0
    return math.exp(-(offset * offset) / (2.0 * spread * spread))


def split_weights(exact):
    high = exact.astype(ml_dtypes.bfloat16)
    low = (exact - high.astype(np.float64)).astype(ml_dtypes.bfloat16)
    return high, low


def level_row_weights(levels, rows, group):
    lev = np.array([[rho(a - b, 2.0) for b in range(levels)] for a in range(levels)])

    def block(shift):
        lat = np.array([[rho(b + shift * rows - a, 2.5) for b in range(rows)] for a in range(rows)])
        return np.kron(np.eye(group), np.kron(lev, lat))

    both = []
    for direct in (1, -1):
        high, low = split_weights(np.concatenate([block(0), block(direct), block(-direct)], axis=1))
        both.append(np.concatenate([high, low], axis=0))
    return np.stack(both)


def kernel(
    group, ahead, owner, fields, held, wlat, out,
    raw, pert, gbuf, gord, cbuf, dbuf, rbuf, total, wide, levelled, give, take,
    p_sem, g_send, g_recv, c_send, c_recv, f_send, f_recv, t_send, t_recv,
):
    members, slots, depth, lon = pert.shape
    holders, _, held_levels, rows, _ = gbuf.shape
    levels = depth // rows
    width = -(-(lon + 2 * REACH) // LANES) * LANES
    after = (width - lon) // 2
    before = width - lon - after

    def field_copy(m):
        return pltpu.make_async_copy(fields.at[m], raw.at[m], p_sem.at[m])

    def start_fields(m, carry):
        field_copy(m).start()
        return carry

    lax.fori_loop(0, members, start_fields, 0)

    me = lax.axis_index("mem")
    here = lax.axis_index("lat")
    count = lax.axis_size("lat")
    parity = lax.rem(here, 2)
    partner = here + 1 - 2 * parity
    hop = 2 - 4 * parity
    target = here + hop
    source = here - hop
    has_target = jnp.logical_and(target >= 0, target < count)
    has_source = jnp.logical_and(source >= 0, source < count)

    barrier = pltpu.get_barrier_semaphore()
    for k in range(1, holders):
        pl.semaphore_signal(
            barrier, inc=1, device_id=(lax.rem(me + k, holders), here), device_id_type=MESH
        )
    pl.semaphore_signal(barrier, inc=1, device_id=(me, partner), device_id_type=MESH)

    @pl.when(has_target)
    def _():
        pl.semaphore_signal(barrier, inc=1, device_id=(me, target), device_id_type=MESH)

    @pl.when(has_source)
    def _():
        pl.semaphore_signal(barrier, inc=1, device_id=(me, source), device_id_type=MESH)

    @pl.when(jnp.logical_not(has_source))
    def _():
        rbuf[...] = jnp.zeros_like(rbuf)

    pl.semaphore_wait(barrier, holders + has_target.astype(jnp.int32) + has_source.astype(jnp.int32))

    def gradient_copy(k):
        return pltpu.make_async_remote_copy(
            src_ref=held, dst_ref=gbuf.at[me],
            send_sem=g_send.at[k - 1], recv_sem=g_recv.at[k - 1],
            device_id=(lax.rem(me + k, holders), here), device_id_type=MESH,
        )

    for k in range(1, holders):
        gradient_copy(k).start()
    gbuf[me] = held[...]
    total[...] = jnp.zeros_like(total)
    for k in range(1, holders):
        gradient_copy(k).wait()

    for level in range(levels):
        place = jnp.int32(0)
        for p in range(levels):
            place = jnp.where(owner[p] == level, p, place)
        holder = lax.div(place, held_levels)
        within = lax.rem(place, held_levels)
        for slot in range(slots):
            gord[slot, level * rows:(level + 1) * rows, :] = gbuf[holder, slot, within]

    def own_copy(m):
        return pltpu.make_async_remote_copy(
            src_ref=cbuf.at[m], dst_ref=dbuf.at[m],
            send_sem=c_send.at[m], recv_sem=c_recv.at[m],
            device_id=(me, partner), device_id_type=MESH,
        )

    def relay_copy(m):
        return pltpu.make_async_remote_copy(
            src_ref=dbuf.at[m], dst_ref=rbuf.at[m],
            send_sem=f_send.at[m], recv_sem=f_recv.at[m],
            device_id=(me, target), device_id_type=MESH,
        )

    def control_step(m, carry):
        field_copy(m).wait()
        value = None
        for slot in range(slots):
            field = jnp.concatenate(
                [raw[m, slot, level].astype(F32) for level in range(levels)], axis=0
            )
            pert[m, slot] = field.astype(BF16)
            term = field * gord[slot]
            value = term if value is None else value + term
        cbuf[m] = value.astype(BF16)
        own_copy(m).start()
        return carry

    lax.fori_loop(0, members, control_step, 0)

    def relay(m):
        own_copy(m).wait_recv()

        @pl.when(has_target)
        def _():
            relay_copy(m).start()

    def process(first):
        @pl.when(has_source)
        def _():
            for i in range(group):
                relay_copy(first + i).wait_recv()

        span = pl.ds(first, group)
        block = group * depth
        stack = jnp.concatenate(
            [buf[span].reshape(block, lon) for buf in (cbuf, dbuf, rbuf)], axis=0
        )
        mixed = jnp.dot(wlat[parity], stack, preferred_element_type=F32)
        mixed = mixed[:block] + mixed[block:]
        wide[...] = jnp.concatenate([mixed, mixed[:, :after], mixed[:, lon - before:]], axis=1)
        for i in range(group):
            ring = wide[i * depth:(i + 1) * depth, :]
            smoothed = rho(0, 3.0) * ring
            for k in range(1, REACH + 1):
                pair = pltpu.roll(ring, k, 1) + pltpu.roll(ring, width - k, 1)
                smoothed = smoothed + rho(k, 3.0) * pair
            smoothed = smoothed[:, :lon]
            for slot in range(slots):
                total[slot] += pert[first + i, slot].astype(F32) * smoothed

    groups = members // group
    lead = min(ahead, groups)

    def relay_group(g):
        for i in range(group):
            relay(g * group + i)

    def relay_step(g, carry):
        relay_group(g)
        return carry

    def step(g, carry):
        relay_group(g + lead)
        process(g * group)
        return carry

    def last_step(g, carry):
        process(g * group)
        return carry

    lax.fori_loop(0, lead, relay_step, 0)
    lax.fori_loop(0, groups - lead, step, 0)
    lax.fori_loop(groups - lead, groups, last_step, 0)

    for level in range(levels):
        for slot in range(slots):
            levelled[slot, level] = total[slot, level * rows:(level + 1) * rows, :]

    def total_copy(k):
        return pltpu.make_async_remote_copy(
            src_ref=give.at[k - 1], dst_ref=take.at[k - 1],
            send_sem=t_send.at[k - 1], recv_sem=t_recv.at[k - 1],
            device_id=(lax.rem(me + k, holders), here), device_id_type=MESH,
        )

    for k in range(1, holders):
        holder = lax.rem(me + k, holders)
        for r in range(held_levels):
            level = owner[holder * held_levels + r]
            for slot in range(slots):
                give[k - 1, slot, r] = levelled[slot, level]
        total_copy(k).start()

    def drain(m, carry):
        own_copy(m).wait_send()

        @pl.when(has_target)
        def _():
            relay_copy(m).wait_send()

        return carry

    lax.fori_loop(0, members, drain, 0)
    for k in range(1, holders):
        total_copy(k).wait()
    for r in range(held_levels):
        level = owner[me * held_levels + r]
        for slot in range(slots):
            value = levelled[slot, level]
            for k in range(1, holders):
                value = value + take[k - 1, slot, r]
            out[slot, r] = value


def local(group, ahead, perturbations, gradient_held, block_owner):
    members, slots, levels, rows, lon = perturbations.shape
    held_levels = gradient_held.shape[1]
    holders = lax.axis_size("mem")
    depth = levels * rows
    others = max(holders - 1, 1)
    width = -(-(lon + 2 * REACH) // LANES) * LANES
    wlat = jnp.asarray(level_row_weights(levels, rows, group))
    vmem = pl.BlockSpec(memory_space=pltpu.VMEM)
    part = (slots, held_levels, rows, lon)
    dma = pltpu.SemaphoreType.DMA
    return pl.pallas_call(
        functools.partial(kernel, group, ahead),
        out_shape=jax.ShapeDtypeStruct(part, F32),
        in_specs=[
            pl.BlockSpec(memory_space=pltpu.SMEM), pl.BlockSpec(memory_space=pltpu.HBM), vmem, vmem,
        ],
        out_specs=vmem,
        scratch_shapes=[
            pltpu.VMEM((members, slots, levels, rows, lon), BF16),
            pltpu.VMEM((members, slots, depth, lon), BF16),
            pltpu.VMEM((holders,) + part, F32),
            pltpu.VMEM((slots, depth, lon), F32),
            pltpu.VMEM((members, depth, lon), BF16),
            pltpu.VMEM((members, depth, lon), BF16),
            pltpu.VMEM((members, depth, lon), BF16),
            pltpu.VMEM((slots, depth, lon), F32),
            pltpu.VMEM((group * depth, width), F32),
            pltpu.VMEM((slots, levels, rows, lon), F32),
            pltpu.VMEM((others,) + part, F32),
            pltpu.VMEM((others,) + part, F32),
            dma((members,)),
            dma((others,)), dma((others,)),
            dma((members,)), dma((members,)),
            dma((members,)), dma((members,)),
            dma((others,)), dma((others,)),
        ],
        compiler_params=pltpu.CompilerParams(
            collective_id=0, has_side_effects=True, vmem_limit_bytes=56 * 1024 * 1024
        ),
    )(
        block_owner, perturbations, gradient_held, wlat,
    )


def solution(mesh):
    placed = (P("mem", None, None, "lat", None), P(None, "mem", "lat", None), P())
    return jax.shard_map(
        functools.partial(local, 2, 2),
        mesh=mesh, in_specs=placed, out_specs=P(None, "mem", "lat", None), check_vma=False,
    )
```

```python
import functools
import math

import jax
import jax.numpy as jnp
import ml_dtypes
import numpy as np
from jax import lax
from jax.experimental import pallas as pl
from jax.experimental.pallas import tpu as pltpu
from jax.sharding import PartitionSpec as P

MESH = pl.DeviceIdType.MESH
REACH = 4
LANES = 128
F32 = jnp.float32
BF16 = jnp.bfloat16


def rho(offset, spread):
    if abs(offset) > REACH:
        return 0.0
    return math.exp(-(offset * offset) / (2.0 * spread * spread))


def split_weights(exact):
    high = exact.astype(ml_dtypes.bfloat16)
    low = (exact - high.astype(np.float64)).astype(ml_dtypes.bfloat16)
    return high, low


def level_row_weights(levels, rows, group):
    lev = np.array([[rho(a - b, 2.0) for b in range(levels)] for a in range(levels)])

    def block(shift):
        lat = np.array([[rho(b + shift * rows - a, 2.5) for b in range(rows)] for a in range(rows)])
        return np.kron(np.eye(group), np.kron(lev, lat))

    both = []
    for direct in (1, -1):
        high, low = split_weights(np.concatenate([block(0), block(direct), block(-direct)], axis=1))
        both.append(np.concatenate([high, low], axis=0))
    return np.stack(both)


def kernel(
    group, ahead, owner, fields, held, wlat, out,
    raw, pert, gbuf, gord, cbuf, dbuf, rbuf, total, wide, levelled, give, take,
    p_sem, g_send, g_recv, c_send, c_recv, f_send, f_recv, t_send, t_recv,
):
    members, slots, depth, lon = pert.shape
    holders, _, held_levels, rows, _ = gbuf.shape
    levels = depth // rows
    width = -(-(lon + 2 * REACH) // LANES) * LANES
    after = (width - lon) // 2
    before = width - lon - after

    def field_copy(m):
        return pltpu.make_async_copy(fields.at[m], raw.at[m], p_sem.at[m])

    def start_fields(m, carry):
        field_copy(m).start()
        return carry

    lax.fori_loop(0, members, start_fields, 0)

    groups = members // group
    early = min(4, groups)

    def convert(m):
        field_copy(m).wait()
        for slot in range(slots):
            pert[m, slot] = jnp.concatenate(
                [raw[m, slot, level].astype(F32) for level in range(levels)], axis=0
            ).astype(BF16)

    def convert_step(m, carry):
        convert(m)
        return carry

    me = lax.axis_index("mem")
    here = lax.axis_index("lat")
    count = lax.axis_size("lat")
    parity = lax.rem(here, 2)
    partner = here + 1 - 2 * parity
    hop = 2 - 4 * parity
    target = here + hop
    source = here - hop
    has_target = jnp.logical_and(target >= 0, target < count)
    has_source = jnp.logical_and(source >= 0, source < count)

    barrier = pltpu.get_barrier_semaphore()
    for k in range(1, holders):
        pl.semaphore_signal(
            barrier, inc=1, device_id=(lax.rem(me + k, holders), here), device_id_type=MESH
        )
    pl.semaphore_signal(barrier, inc=1, device_id=(me, partner), device_id_type=MESH)

    @pl.when(has_target)
    def _():
        pl.semaphore_signal(barrier, inc=1, device_id=(me, target), device_id_type=MESH)

    @pl.when(has_source)
    def _():
        pl.semaphore_signal(barrier, inc=1, device_id=(me, source), device_id_type=MESH)

    @pl.when(jnp.logical_not(has_source))
    def _():
        rbuf[...] = jnp.zeros_like(rbuf)

    half = early * group // 2
    lax.fori_loop(0, half, convert_step, 0)
    pl.semaphore_wait(barrier, holders + has_target.astype(jnp.int32) + has_source.astype(jnp.int32))

    def gradient_copy(k):
        return pltpu.make_async_remote_copy(
            src_ref=held, dst_ref=gbuf.at[me],
            send_sem=g_send.at[k - 1], recv_sem=g_recv.at[k - 1],
            device_id=(lax.rem(me + k, holders), here), device_id_type=MESH,
        )

    for k in range(1, holders):
        gradient_copy(k).start()
    gbuf[me] = held[...]
    total[...] = jnp.zeros_like(total)
    lax.fori_loop(half, early * group, convert_step, 0)
    for k in range(1, holders):
        gradient_copy(k).wait()

    for level in range(levels):
        place = jnp.int32(0)
        for p in range(levels):
            place = jnp.where(owner[p] == level, p, place)
        holder = lax.div(place, held_levels)
        within = lax.rem(place, held_levels)
        for slot in range(slots):
            gord[slot, level * rows:(level + 1) * rows, :] = gbuf[holder, slot, within]

    def own_copy(m):
        return pltpu.make_async_remote_copy(
            src_ref=cbuf.at[m], dst_ref=dbuf.at[m],
            send_sem=c_send.at[m], recv_sem=c_recv.at[m],
            device_id=(me, partner), device_id_type=MESH,
        )

    def relay_copy(m):
        return pltpu.make_async_remote_copy(
            src_ref=dbuf.at[m], dst_ref=rbuf.at[m],
            send_sem=f_send.at[m], recv_sem=f_recv.at[m],
            device_id=(me, target), device_id_type=MESH,
        )

    def control(m):
        value = None
        for slot in range(slots):
            term = pert[m, slot].astype(F32) * gord[slot]
            value = term if value is None else value + term
        cbuf[m] = value.astype(BF16)
        own_copy(m).start()

    def relay(m):
        own_copy(m).wait_recv()

        @pl.when(has_target)
        def _():
            relay_copy(m).start()

    def process(first):
        @pl.when(has_source)
        def _():
            for i in range(group):
                relay_copy(first + i).wait_recv()

        span = pl.ds(first, group)
        block = group * depth
        stack = jnp.concatenate(
            [buf[span].reshape(block, lon) for buf in (cbuf, dbuf, rbuf)], axis=0
        )
        mixed = jnp.dot(wlat[parity], stack, preferred_element_type=F32)
        mixed = mixed[:block] + mixed[block:]
        wide[...] = jnp.concatenate([mixed, mixed[:, :after], mixed[:, lon - before:]], axis=1)
        for i in range(group):
            ring = wide[i * depth:(i + 1) * depth, :]
            smoothed = rho(0, 3.0) * ring
            for k in range(1, REACH + 1):
                pair = pltpu.roll(ring, k, 1) + pltpu.roll(ring, width - k, 1)
                smoothed = smoothed + rho(k, 3.0) * pair
            smoothed = smoothed[:, :lon]
            for slot in range(slots):
                total[slot] += pert[first + i, slot].astype(F32) * smoothed

    def stage(first, last, convert_on, control_on, relay_on, process_on):
        def step(g, carry):
            for i in range(group):
                if control_on:
                    control(g * group + i)
                if convert_on:
                    convert((g + early) * group + i)
            for i in range(group):
                if relay_on:
                    relay((g - ahead) * group + i)
            if process_on:
                process((g - 2 * ahead) * group)
            return carry

        if first < last:
            lax.fori_loop(first, last, step, 0)

    bounds = sorted({0, ahead, 2 * ahead, groups - early, groups, groups + ahead, groups + 2 * ahead})
    for first, last in zip(bounds[:-1], bounds[1:]):
        stage(
            first, last, first < groups - early, first < groups,
            ahead <= first < groups + ahead, 2 * ahead <= first,
        )

    for level in range(levels):
        for slot in range(slots):
            levelled[slot, level] = total[slot, level * rows:(level + 1) * rows, :]

    def total_copy(k):
        return pltpu.make_async_remote_copy(
            src_ref=give.at[k - 1], dst_ref=take.at[k - 1],
            send_sem=t_send.at[k - 1], recv_sem=t_recv.at[k - 1],
            device_id=(lax.rem(me + k, holders), here), device_id_type=MESH,
        )

    for k in range(1, holders):
        holder = lax.rem(me + k, holders)
        for r in range(held_levels):
            level = owner[holder * held_levels + r]
            for slot in range(slots):
                give[k - 1, slot, r] = levelled[slot, level]
        total_copy(k).start()

    def drain(m, carry):
        own_copy(m).wait_send()

        @pl.when(has_target)
        def _():
            relay_copy(m).wait_send()

        return carry

    lax.fori_loop(0, members, drain, 0)
    for k in range(1, holders):
        total_copy(k).wait()
    for r in range(held_levels):
        level = owner[me * held_levels + r]
        for slot in range(slots):
            value = levelled[slot, level]
            for k in range(1, holders):
                value = value + take[k - 1, slot, r]
            out[slot, r] = value


def local(group, ahead, perturbations, gradient_held, block_owner):
    members, slots, levels, rows, lon = perturbations.shape
    held_levels = gradient_held.shape[1]
    holders = lax.axis_size("mem")
    depth = levels * rows
    others = max(holders - 1, 1)
    width = -(-(lon + 2 * REACH) // LANES) * LANES
    wlat = jnp.asarray(level_row_weights(levels, rows, group))
    vmem = pl.BlockSpec(memory_space=pltpu.VMEM)
    part = (slots, held_levels, rows, lon)
    dma = pltpu.SemaphoreType.DMA
    return pl.pallas_call(
        functools.partial(kernel, group, ahead),
        out_shape=jax.ShapeDtypeStruct(part, F32),
        in_specs=[
            pl.BlockSpec(memory_space=pltpu.SMEM), pl.BlockSpec(memory_space=pltpu.HBM), vmem, vmem,
        ],
        out_specs=vmem,
        scratch_shapes=[
            pltpu.VMEM((members, slots, levels, rows, lon), BF16),
            pltpu.VMEM((members, slots, depth, lon), BF16),
            pltpu.VMEM((holders,) + part, F32),
            pltpu.VMEM((slots, depth, lon), F32),
            pltpu.VMEM((members, depth, lon), BF16),
            pltpu.VMEM((members, depth, lon), BF16),
            pltpu.VMEM((members, depth, lon), BF16),
            pltpu.VMEM((slots, depth, lon), F32),
            pltpu.VMEM((group * depth, width), F32),
            pltpu.VMEM((slots, levels, rows, lon), F32),
            pltpu.VMEM((others,) + part, F32),
            pltpu.VMEM((others,) + part, F32),
            dma((members,)),
            dma((others,)), dma((others,)),
            dma((members,)), dma((members,)),
            dma((members,)), dma((members,)),
            dma((others,)), dma((others,)),
        ],
        compiler_params=pltpu.CompilerParams(
            collective_id=0, has_side_effects=True, vmem_limit_bytes=53 * 1024 * 1024
        ),
    )(
        block_owner, perturbations, gradient_held, wlat,
    )


def solution(mesh):
    placed = (P("mem", None, None, "lat", None), P(None, "mem", "lat", None), P())
    return jax.shard_map(
        functools.partial(local, 2, 2),
        mesh=mesh, in_specs=placed, out_specs=P(None, "mem", "lat", None), check_vma=False,
    )
```

```python
import functools
import math

import jax
import jax.numpy as jnp
from jax import lax
from jax.experimental import pallas as pl
from jax.experimental.pallas import tpu as pltpu
from jax.sharding import PartitionSpec as P

MESH = pl.DeviceIdType.MESH
REACH = 4
LANES = 128
PAIR = 2
AHEAD = 2
F32 = jnp.float32
BF16 = jnp.bfloat16


def rho(offset, spread):
    return math.exp(-(offset * offset) / (2.0 * spread * spread))


def rho_of(apart, spread):
    value = jnp.zeros(apart.shape, F32)
    for a in range(REACH + 1):
        value = jnp.where(jnp.abs(apart) == a, rho(a, spread), value)
    return value


def fill_mixing(weights, owner, holders, held_levels, rows, direct):
    inner = PAIR * held_levels * rows
    block = holders * inner

    def places(axis):
        index = lax.broadcasted_iota(jnp.int32, (block, 3 * block), axis)
        part = jnp.where(index >= block, 1, 0) + jnp.where(index >= 2 * block, 1, 0)
        index = index - part * block
        level = jnp.zeros_like(index)
        member = jnp.zeros_like(index)
        row = index
        for p in range(holders * held_levels):
            for i in range(PAIR):
                start = (p // held_levels) * inner + (i * held_levels + p % held_levels) * rows
                inside = jnp.logical_and(index >= start, index < start + rows)
                level = jnp.where(inside, owner[p], level)
                member = jnp.where(inside, i, member)
                row = jnp.where(inside, index - start, row)
        shift = jnp.where(part == 1, direct, jnp.where(part == 2, -direct, 0))
        return level, member, row + shift * rows

    to_level, to_member, to_row = places(0)
    from_level, from_member, from_row = places(1)
    exact = rho_of(from_level - to_level, 2.0) * rho_of(from_row - to_row, 2.5)
    exact = jnp.where(from_member == to_member, exact, 0.0)
    high = exact.astype(BF16)
    weights[:block, :] = high
    weights[block:, :] = (exact - high.astype(F32)).astype(BF16)


def kernel(
    owner, fields, held, out,
    raw, pert, gbuf, grad, cbuf, dbuf, rbuf, weights, wide, total, give, take,
    p_sem, g_send, g_recv, c_send, c_recv, f_send, f_recv, t_send, t_recv,
):
    members, slots, levels, rows, lon = fields.shape
    held_levels = held.shape[1]
    holders = levels // held_levels
    pairs = members // PAIR
    inner = PAIR * held_levels * rows
    block = holders * inner
    half = held_levels * rows
    width = wide.shape[1]
    after = (width - lon) // 2
    before = width - lon - after
    early = min(AHEAD, pairs)

    fetch = pltpu.make_async_copy(fields, raw, p_sem.at[0])
    fetch.start()

    me = lax.axis_index("mem")
    here = lax.axis_index("lat")
    count = lax.axis_size("lat")
    parity = lax.rem(here, 2)
    partner = here + 1 - 2 * parity
    hop = 2 - 4 * parity
    target = here + hop
    source = here - hop
    has_target = jnp.logical_and(target >= 0, target < count)
    has_source = jnp.logical_and(source >= 0, source < count)

    barrier = pltpu.get_barrier_semaphore()
    for k in range(1, holders):
        pl.semaphore_signal(
            barrier, inc=1, device_id=(lax.rem(me + k, holders), here), device_id_type=MESH
        )
    pl.semaphore_signal(barrier, inc=1, device_id=(me, partner), device_id_type=MESH)

    @pl.when(has_target)
    def _():
        pl.semaphore_signal(barrier, inc=1, device_id=(me, target), device_id_type=MESH)

    @pl.when(has_source)
    def _():
        pl.semaphore_signal(barrier, inc=1, device_id=(me, source), device_id_type=MESH)

    def gradient_copy(k):
        return pltpu.make_async_remote_copy(
            src_ref=held, dst_ref=gbuf.at[me],
            send_sem=g_send.at[k - 1], recv_sem=g_recv.at[k - 1],
            device_id=(lax.rem(me + k, holders), here), device_id_type=MESH,
        )

    def own_copy(g, holder):
        return pltpu.make_async_remote_copy(
            src_ref=cbuf.at[g, holder], dst_ref=dbuf.at[g, holder],
            send_sem=c_send.at[g, holder], recv_sem=c_recv.at[g, holder],
            device_id=(me, partner), device_id_type=MESH,
        )

    def relay_copy(g, holder):
        return pltpu.make_async_remote_copy(
            src_ref=dbuf.at[g, holder], dst_ref=rbuf.at[g, holder],
            send_sem=f_send.at[g, holder], recv_sem=f_recv.at[g, holder],
            device_id=(me, target), device_id_type=MESH,
        )

    def convert(g, carry=0):
        for slot in range(slots):
            for holder in range(holders):
                pieces = [
                    raw[g * PAIR + i, slot, owner[holder * held_levels + r]].astype(F32)
                    for i in range(PAIR) for r in range(held_levels)
                ]
                pert[g, slot, holder] = jnp.concatenate(pieces, axis=0).astype(BF16)
        return carry

    def place_gradient(holder, block_ref):
        for slot in range(slots):
            pieces = [block_ref[slot, r] for r in range(held_levels)] * PAIR
            grad[slot, holder] = jnp.concatenate(pieces, axis=0)

    def control(g, holder):
        value = None
        for slot in range(slots):
            term = pert[g, slot, holder].astype(F32) * grad[slot, holder]
            value = term if value is None else value + term
        cbuf[g, holder] = value.astype(BF16)

    place_gradient(me, held)
    fetch.wait()
    for g in range(early):
        convert(g)
        control(g, me)

    pl.semaphore_wait(barrier, holders + has_target.astype(jnp.int32) + has_source.astype(jnp.int32))
    for k in range(1, holders):
        gradient_copy(k).start()
    for g in range(early):
        own_copy(g, me).start()

    @pl.when(jnp.logical_not(has_source))
    def _():
        rbuf[...] = jnp.zeros_like(rbuf)

    for k in range(1, holders):
        gradient_copy(k).wait_recv()
        holder = lax.rem(me + holders - k, holders)
        place_gradient(holder, gbuf.at[holder])

    for g in range(early):
        for k in range(1, holders):
            holder = lax.rem(me + k, holders)
            control(g, holder)
            own_copy(g, holder).start()

    total[...] = jnp.zeros_like(total)

    def send(g):
        convert(g)
        for k in range(holders):
            holder = lax.rem(me + k, holders)
            control(g, holder)
            own_copy(g, holder).start()

    def relay(g):
        for k in range(holders):
            holder = lax.rem(me + k, holders)
            own_copy(g, holder).wait_recv()

            @pl.when(has_target)
            def _():
                relay_copy(g, holder).start()

    def process(g):
        @pl.when(has_source)
        def _():
            for holder in range(holders):
                relay_copy(g, holder).wait_recv()

        stack = jnp.concatenate(
            [buf[g].reshape(block, lon) for buf in (cbuf, dbuf, rbuf)], axis=0
        )
        mixed = jnp.dot(weights[...], stack, preferred_element_type=F32)
        mixed = mixed[:block] + mixed[block:]
        wide[...] = jnp.concatenate([mixed, mixed[:, :after], mixed[:, lon - before:]], axis=1)
        for holder in range(holders):
            ring = wide[holder * inner:(holder + 1) * inner, :]
            smoothed = rho(0, 3.0) * ring
            for k in range(1, REACH + 1):
                both = pltpu.roll(ring, k, 1) + pltpu.roll(ring, width - k, 1)
                smoothed = smoothed + rho(k, 3.0) * both
            smoothed = smoothed[:, :lon]
            for slot in range(slots):
                total[slot, holder] += pert[g, slot, holder].astype(F32) * smoothed

    def stage(first, last, send_on, relay_on, process_on):
        def step(g, carry):
            if send_on:
                send(g)
            if relay_on:
                relay(g - AHEAD)
            if process_on:
                process(g - 2 * AHEAD)
            return carry

        if first < last:
            lax.fori_loop(first, last, step, 0)

    stage(early, early + 1, True, False, False)
    fill_mixing(weights, owner, holders, held_levels, rows, 1 - 2 * parity)
    relay(0)
    stage(early + 1, 2 * AHEAD, True, True, False)
    stage(2 * AHEAD, pairs, True, True, True)
    stage(pairs, pairs + AHEAD, False, True, True)
    stage(pairs + AHEAD, pairs + 2 * AHEAD, False, False, True)

    def total_copy(k):
        return pltpu.make_async_remote_copy(
            src_ref=give.at[k - 1], dst_ref=take.at[k - 1],
            send_sem=t_send.at[k - 1], recv_sem=t_recv.at[k - 1],
            device_id=(lax.rem(me + k, holders), here), device_id_type=MESH,
        )

    for k in range(1, holders):
        holder = lax.rem(me + k, holders)
        for slot in range(slots):
            full = total[slot, holder]
            give[k - 1, slot] = sum(full[i * half:(i + 1) * half] for i in range(1, PAIR)) + full[:half]
        total_copy(k).start()

    for k in range(1, holders):
        gradient_copy(k).wait_send()

    def drain(g, carry):
        for holder in range(holders):
            own_copy(g, holder).wait_send()

            @pl.when(has_target)
            def _():
                relay_copy(g, holder).wait_send()

        return carry

    lax.fori_loop(0, pairs, drain, 0)
    for k in range(1, holders):
        total_copy(k).wait()
    for slot in range(slots):
        full = total[slot, me]
        value = sum(full[i * half:(i + 1) * half] for i in range(1, PAIR)) + full[:half]
        for k in range(1, holders):
            value = value + take[k - 1, slot]
        for r in range(held_levels):
            out[slot, r] = value[r * rows:(r + 1) * rows]


def local(perturbations, gradient_held, block_owner):
    members, slots, levels, rows, lon = perturbations.shape
    held_levels = gradient_held.shape[1]
    holders = levels // held_levels
    pairs = members // PAIR
    inner = PAIR * held_levels * rows
    block = holders * inner
    others = max(holders - 1, 1)
    width = -(-(lon + 2 * REACH) // LANES) * LANES
    part = (slots, held_levels, rows, lon)
    dma = pltpu.SemaphoreType.DMA
    return pl.pallas_call(
        kernel,
        out_shape=jax.ShapeDtypeStruct(part, F32),
        in_specs=[
            pl.BlockSpec(memory_space=pltpu.SMEM),
            pl.BlockSpec(memory_space=pltpu.HBM),
            pl.BlockSpec(memory_space=pltpu.VMEM),
        ],
        out_specs=pl.BlockSpec(memory_space=pltpu.VMEM),
        scratch_shapes=[
            pltpu.VMEM((members, slots, levels, rows, lon), BF16),
            pltpu.VMEM((pairs, slots, holders, inner, lon), BF16),
            pltpu.VMEM((holders,) + part, F32),
            pltpu.VMEM((slots, holders, inner, lon), F32),
            pltpu.VMEM((pairs, holders, inner, lon), BF16),
            pltpu.VMEM((pairs, holders, inner, lon), BF16),
            pltpu.VMEM((pairs, holders, inner, lon), BF16),
            pltpu.VMEM((2 * block, 3 * block), BF16),
            pltpu.VMEM((block, width), F32),
            pltpu.VMEM((slots, holders, inner, lon), F32),
            pltpu.VMEM((others, slots, held_levels * rows, lon), F32),
            pltpu.VMEM((others, slots, held_levels * rows, lon), F32),
            dma((1,)),
            dma((others,)), dma((others,)),
            dma((pairs, holders)), dma((pairs, holders)),
            dma((pairs, holders)), dma((pairs, holders)),
            dma((others,)), dma((others,)),
        ],
        compiler_params=pltpu.CompilerParams(
            collective_id=0, has_side_effects=True, vmem_limit_bytes=538 * 1024 * 1024 // 10
        ),
    )(block_owner, perturbations, gradient_held)


def solution(mesh):
    placed = (P("mem", None, None, "lat", None), P(None, "mem", "lat", None), P())
    return jax.shard_map(
        local, mesh=mesh, in_specs=placed, out_specs=P(None, "mem", "lat", None), check_vma=False,
    )
```

```python
import functools
import math

import jax
import jax.numpy as jnp
from jax import lax
from jax.experimental import pallas as pl
from jax.experimental.pallas import tpu as pltpu
from jax.sharding import PartitionSpec as P

MESH = pl.DeviceIdType.MESH
REACH = 4
LANES = 128
PAIR = 2
AHEAD = 2
F32 = jnp.float32
BF16 = jnp.bfloat16


def rho(offset, spread):
    return math.exp(-(offset * offset) / (2.0 * spread * spread))


def rho_of(apart, spread):
    value = jnp.zeros(apart.shape, F32)
    for a in range(REACH + 1):
        value = jnp.where(jnp.abs(apart) == a, rho(a, spread), value)
    return value


def fill_mixing(weights, owner, holders, held_levels, rows, direct):
    inner = PAIR * held_levels * rows
    block = holders * inner

    def places(axis):
        index = lax.broadcasted_iota(jnp.int32, (block, 3 * block), axis)
        part = jnp.where(index >= block, 1, 0) + jnp.where(index >= 2 * block, 1, 0)
        index = index - part * block
        level = jnp.zeros_like(index)
        member = jnp.zeros_like(index)
        row = index
        for p in range(holders * held_levels):
            for i in range(PAIR):
                start = (p // held_levels) * inner + (i * held_levels + p % held_levels) * rows
                inside = jnp.logical_and(index >= start, index < start + rows)
                level = jnp.where(inside, owner[p], level)
                member = jnp.where(inside, i, member)
                row = jnp.where(inside, index - start, row)
        shift = jnp.where(part == 1, direct, jnp.where(part == 2, -direct, 0))
        return level, member, row + shift * rows

    to_level, to_member, to_row = places(0)
    from_level, from_member, from_row = places(1)
    exact = rho_of(from_level - to_level, 2.0) * rho_of(from_row - to_row, 2.5)
    exact = jnp.where(from_member == to_member, exact, 0.0)
    high = exact.astype(BF16)
    weights[:block, :] = high
    weights[block:, :] = (exact - high.astype(F32)).astype(BF16)


def kernel(
    owner, fields, held, out,
    raw, pert, gbuf, grad, cbuf, dbuf, rbuf, ctail, dtail, rtail, weights, last, wide, total, give, take,
    p_sem, g_send, g_recv, c_send, c_recv, f_send, f_recv,
    ct_send, ct_recv, ft_send, ft_recv, t_send, t_recv,
):
    members, slots, levels, rows, lon = fields.shape
    held_levels = held.shape[1]
    holders = levels // held_levels
    pairs = members // PAIR
    inner = PAIR * held_levels * rows
    block = holders * inner
    half = held_levels * rows
    width = wide.shape[1]
    main = cbuf.shape[-1]
    rest = lon - main
    share = LANES // rest
    quads = pairs // share
    after = (width - lon) // 2
    before = width - lon - after - rest
    early = min(AHEAD, pairs)

    fetch = pltpu.make_async_copy(fields, raw, p_sem.at[0])
    fetch.start()

    me = lax.axis_index("mem")
    here = lax.axis_index("lat")
    count = lax.axis_size("lat")
    parity = lax.rem(here, 2)
    partner = here + 1 - 2 * parity
    hop = 2 - 4 * parity
    target = here + hop
    source = here - hop
    has_target = jnp.logical_and(target >= 0, target < count)
    has_source = jnp.logical_and(source >= 0, source < count)

    barrier = pltpu.get_barrier_semaphore()
    for k in range(1, holders):
        pl.semaphore_signal(
            barrier, inc=1, device_id=(lax.rem(me + k, holders), here), device_id_type=MESH
        )
    pl.semaphore_signal(barrier, inc=1, device_id=(me, partner), device_id_type=MESH)

    @pl.when(has_target)
    def _():
        pl.semaphore_signal(barrier, inc=1, device_id=(me, target), device_id_type=MESH)

    @pl.when(has_source)
    def _():
        pl.semaphore_signal(barrier, inc=1, device_id=(me, source), device_id_type=MESH)

    def gradient_copy(k):
        return pltpu.make_async_remote_copy(
            src_ref=held, dst_ref=gbuf.at[me],
            send_sem=g_send.at[k - 1], recv_sem=g_recv.at[k - 1],
            device_id=(lax.rem(me + k, holders), here), device_id_type=MESH,
        )

    def own_copy(g, holder):
        return pltpu.make_async_remote_copy(
            src_ref=cbuf.at[g, holder], dst_ref=dbuf.at[g, holder],
            send_sem=c_send.at[g, holder], recv_sem=c_recv.at[g, holder],
            device_id=(me, partner), device_id_type=MESH,
        )

    def relay_copy(g, holder):
        return pltpu.make_async_remote_copy(
            src_ref=dbuf.at[g, holder], dst_ref=rbuf.at[g, holder],
            send_sem=f_send.at[g, holder], recv_sem=f_recv.at[g, holder],
            device_id=(me, target), device_id_type=MESH,
        )

    def own_tail(q, holder):
        return pltpu.make_async_remote_copy(
            src_ref=ctail.at[q, holder], dst_ref=dtail.at[q, holder],
            send_sem=ct_send.at[q, holder], recv_sem=ct_recv.at[q, holder],
            device_id=(me, partner), device_id_type=MESH,
        )

    def relay_tail(q, holder):
        return pltpu.make_async_remote_copy(
            src_ref=dtail.at[q, holder], dst_ref=rtail.at[q, holder],
            send_sem=ft_send.at[q, holder], recv_sem=ft_recv.at[q, holder],
            device_id=(me, target), device_id_type=MESH,
        )

    def convert(g, carry=0):
        for slot in range(slots):
            for holder in range(holders):
                pieces = [
                    raw[g * PAIR + i, slot, owner[holder * held_levels + r]].astype(F32)
                    for i in range(PAIR) for r in range(held_levels)
                ]
                pert[g, slot, holder] = jnp.concatenate(pieces, axis=0).astype(BF16)
        return carry

    def place_gradient(holder, block_ref):
        for slot in range(slots):
            pieces = [block_ref[slot, r] for r in range(held_levels)] * PAIR
            grad[slot, holder] = jnp.concatenate(pieces, axis=0)

    def product(g, holder, lanes):
        value = None
        for slot in range(slots):
            term = pert[g, slot, holder, :, lanes].astype(F32) * grad[slot, holder, :, lanes]
            value = term if value is None else value + term
        return value

    def control(g, holder):
        cbuf[g, holder] = product(g, holder, slice(0, main)).astype(BF16)

    place_gradient(me, held)
    fetch.wait()
    convert(0)
    control(0, me)
    pl.semaphore_wait(barrier, holders + has_target.astype(jnp.int32) + has_source.astype(jnp.int32))
    for k in range(1, holders):
        gradient_copy(k).start()
    own_copy(0, me).start()
    for g in range(1, early):
        convert(g)
        control(g, me)
        own_copy(g, me).start()

    @pl.when(jnp.logical_not(has_source))
    def _():
        rbuf[...] = jnp.zeros_like(rbuf)
        rtail[...] = jnp.zeros_like(rtail)

    for k in range(1, holders):
        gradient_copy(k).wait_recv()
        holder = lax.rem(me + holders - k, holders)
        place_gradient(holder, gbuf.at[holder])

    for g in range(early):
        for k in range(1, holders):
            holder = lax.rem(me + k, holders)
            control(g, holder)
            own_copy(g, holder).start()

    total[...] = jnp.zeros_like(total)

    lax.fori_loop(early, pairs, convert, 0)
    for q in range(quads):
        for holder in range(holders):
            tails = [product(q * share + j, holder, slice(main, lon)) for j in range(share)]
            ctail[q, holder] = jnp.concatenate(tails, axis=1).astype(BF16)
            own_tail(q, holder).start()

    def send(g):
        for k in range(holders):
            holder = lax.rem(me + k, holders)
            control(g, holder)
            own_copy(g, holder).start()

    def relay(g):
        for k in range(holders):
            holder = lax.rem(me + k, holders)
            own_copy(g, holder).wait_recv()

            @pl.when(has_target)
            def _():
                relay_copy(g, holder).start()

    def mix(stack):
        mixed = jnp.dot(weights[...], stack, preferred_element_type=F32)
        return mixed[:block] + mixed[block:]

    def mix_tails():
        @pl.when(has_source)
        def _():
            for q in range(quads):
                for holder in range(holders):
                    relay_tail(q, holder).wait_recv()

        for q in range(quads):
            stack = jnp.concatenate(
                [buf[q].reshape(block, LANES) for buf in (ctail, dtail, rtail)], axis=0
            )
            mixed = mix(stack)
            for j in range(share):
                last[q * share + j] = mixed[:, j * rest:(j + 1) * rest]

    def process(g):
        @pl.when(has_source)
        def _():
            for holder in range(holders):
                relay_copy(g, holder).wait_recv()

        stack = jnp.concatenate(
            [buf[g].reshape(block, main) for buf in (cbuf, dbuf, rbuf)], axis=0
        )
        mixed = mix(stack)
        wide[:, :main] = mixed
        tail = last[g]
        wide[:, main:] = jnp.concatenate(
            [tail, mixed[:, :after], mixed[:, main - before:], tail], axis=1
        )
        for holder in range(holders):
            ring = wide[holder * inner:(holder + 1) * inner, :]
            smoothed = rho(0, 3.0) * ring
            for k in range(1, REACH + 1):
                both = pltpu.roll(ring, k, 1) + pltpu.roll(ring, width - k, 1)
                smoothed = smoothed + rho(k, 3.0) * both
            smoothed = smoothed[:, :lon]
            for slot in range(slots):
                total[slot, holder] += pert[g, slot, holder].astype(F32) * smoothed

    def stage(first, last, send_on, relay_on, process_on):
        def step(g, carry):
            if send_on:
                send(g)
            if relay_on:
                relay(g - AHEAD)
            if process_on:
                process(g - 2 * AHEAD)
            return carry

        if first < last:
            lax.fori_loop(first, last, step, 0)

    stage(early, early + 1, True, False, False)
    fill_mixing(weights, owner, holders, held_levels, rows, 1 - 2 * parity)
    relay(0)
    stage(early + 1, 2 * AHEAD, True, True, False)
    for q in range(quads):
        for holder in range(holders):
            own_tail(q, holder).wait_recv()

            @pl.when(has_target)
            def _():
                relay_tail(q, holder).start()

    stage(2 * AHEAD, 2 * AHEAD + 1, True, True, False)
    mix_tails()
    process(0)
    stage(2 * AHEAD + 1, pairs, True, True, True)
    stage(pairs, pairs + AHEAD, False, True, True)
    stage(pairs + AHEAD, pairs + 2 * AHEAD, False, False, True)

    def total_copy(k):
        return pltpu.make_async_remote_copy(
            src_ref=give.at[k - 1], dst_ref=take.at[k - 1],
            send_sem=t_send.at[k - 1], recv_sem=t_recv.at[k - 1],
            device_id=(lax.rem(me + k, holders), here), device_id_type=MESH,
        )

    for k in range(1, holders):
        holder = lax.rem(me + k, holders)
        for slot in range(slots):
            full = total[slot, holder]
            give[k - 1, slot] = sum(full[i * half:(i + 1) * half] for i in range(1, PAIR)) + full[:half]
        total_copy(k).start()

    for k in range(1, holders):
        gradient_copy(k).wait_send()

    def drain(g, carry):
        for holder in range(holders):
            own_copy(g, holder).wait_send()

            @pl.when(has_target)
            def _():
                relay_copy(g, holder).wait_send()

        return carry

    lax.fori_loop(0, pairs, drain, 0)
    for q in range(quads):
        for holder in range(holders):
            own_tail(q, holder).wait_send()

            @pl.when(has_target)
            def _():
                relay_tail(q, holder).wait_send()

    for k in range(1, holders):
        total_copy(k).wait()
    for slot in range(slots):
        full = total[slot, me]
        value = sum(full[i * half:(i + 1) * half] for i in range(1, PAIR)) + full[:half]
        for k in range(1, holders):
            value = value + take[k - 1, slot]
        for r in range(held_levels):
            out[slot, r] = value[r * rows:(r + 1) * rows]


def local(perturbations, gradient_held, block_owner):
    members, slots, levels, rows, lon = perturbations.shape
    held_levels = gradient_held.shape[1]
    holders = levels // held_levels
    pairs = members // PAIR
    inner = PAIR * held_levels * rows
    block = holders * inner
    others = max(holders - 1, 1)
    width = -(-(lon + 2 * REACH) // LANES) * LANES
    main = lon // LANES * LANES
    rest = lon - main
    share = LANES // rest
    quads = pairs // share
    part = (slots, held_levels, rows, lon)
    dma = pltpu.SemaphoreType.DMA
    return pl.pallas_call(
        kernel,
        out_shape=jax.ShapeDtypeStruct(part, F32),
        in_specs=[
            pl.BlockSpec(memory_space=pltpu.SMEM),
            pl.BlockSpec(memory_space=pltpu.HBM),
            pl.BlockSpec(memory_space=pltpu.VMEM),
        ],
        out_specs=pl.BlockSpec(memory_space=pltpu.VMEM),
        scratch_shapes=[
            pltpu.VMEM((members, slots, levels, rows, lon), BF16),
            pltpu.VMEM((pairs, slots, holders, inner, lon), BF16),
            pltpu.VMEM((holders,) + part, F32),
            pltpu.VMEM((slots, holders, inner, lon), F32),
            pltpu.VMEM((pairs, holders, inner, main), BF16),
            pltpu.VMEM((pairs, holders, inner, main), BF16),
            pltpu.VMEM((pairs, holders, inner, main), BF16),
            pltpu.VMEM((quads, holders, inner, LANES), BF16),
            pltpu.VMEM((quads, holders, inner, LANES), BF16),
            pltpu.VMEM((quads, holders, inner, LANES), BF16),
            pltpu.VMEM((2 * block, 3 * block), BF16),
            pltpu.VMEM((pairs, block, rest), F32),
            pltpu.VMEM((block, width), F32),
            pltpu.VMEM((slots, holders, inner, lon), F32),
            pltpu.VMEM((others, slots, held_levels * rows, lon), F32),
            pltpu.VMEM((others, slots, held_levels * rows, lon), F32),
            dma((1,)),
            dma((others,)), dma((others,)),
            dma((pairs, holders)), dma((pairs, holders)),
            dma((pairs, holders)), dma((pairs, holders)),
            dma((quads, holders)), dma((quads, holders)),
            dma((quads, holders)), dma((quads, holders)),
            dma((others,)), dma((others,)),
        ],
        compiler_params=pltpu.CompilerParams(
            collective_id=0, has_side_effects=True, vmem_limit_bytes=538 * 1024 * 1024 // 10
        ),
    )(block_owner, perturbations, gradient_held)


def solution(mesh):
    placed = (P("mem", None, None, "lat", None), P(None, "mem", "lat", None), P())
    return jax.shard_map(
        local, mesh=mesh, in_specs=placed, out_specs=P(None, "mem", "lat", None), check_vma=False,
    )
```

```python
import functools
import math

import jax
import jax.numpy as jnp
from jax import lax
from jax.experimental import pallas as pl
from jax.experimental.pallas import tpu as pltpu
from jax.sharding import PartitionSpec as P

MESH = pl.DeviceIdType.MESH
REACH = 4
LANES = 128
PAIR = 2
AHEAD = 2
LAG = 3
F32 = jnp.float32
BF16 = jnp.bfloat16


def rho(offset, spread):
    return math.exp(-(offset * offset) / (2.0 * spread * spread))


def rho_of(apart, spread):
    value = jnp.zeros(apart.shape, F32)
    for a in range(REACH + 1):
        value = jnp.where(jnp.abs(apart) == a, rho(a, spread), value)
    return value


def fill_mixing(weights, owner, holders, held_levels, rows, direct):
    inner = PAIR * held_levels * rows
    block = holders * inner

    def places(axis):
        index = lax.broadcasted_iota(jnp.int32, (block, 3 * block), axis)
        part = jnp.where(index >= block, 1, 0) + jnp.where(index >= 2 * block, 1, 0)
        index = index - part * block
        level = jnp.zeros_like(index)
        member = jnp.zeros_like(index)
        row = index
        for p in range(holders * held_levels):
            for i in range(PAIR):
                start = (p // held_levels) * inner + (i * held_levels + p % held_levels) * rows
                inside = jnp.logical_and(index >= start, index < start + rows)
                level = jnp.where(inside, owner[p], level)
                member = jnp.where(inside, i, member)
                row = jnp.where(inside, index - start, row)
        shift = jnp.where(part == 1, direct, jnp.where(part == 2, -direct, 0))
        return level, member, row + shift * rows

    to_level, to_member, to_row = places(0)
    from_level, from_member, from_row = places(1)
    exact = rho_of(from_level - to_level, 2.0) * rho_of(from_row - to_row, 2.5)
    exact = jnp.where(from_member == to_member, exact, 0.0)
    high = exact.astype(BF16)
    weights[:block, :] = high
    weights[block:, :] = (exact - high.astype(F32)).astype(BF16)


def kernel(
    owner, fields, held, out,
    raw, pert, gbuf, grad, cbuf, dbuf, rbuf, ctail, dtail, rtail, weights, last, wide, total, give, take,
    p_sem, g_send, g_recv, c_send, c_recv, f_send, f_recv,
    ct_send, ct_recv, ft_send, ft_recv, t_send, t_recv,
):
    members, slots, levels, rows, lon = fields.shape
    held_levels = held.shape[1]
    holders = levels // held_levels
    pairs = members // PAIR
    inner = PAIR * held_levels * rows
    block = holders * inner
    half = held_levels * rows
    width = wide.shape[1]
    main = cbuf.shape[-1]
    rest = lon - main
    share = LANES // rest
    quads = pairs // share
    after = (width - lon) // 2
    before = width - lon - after - rest
    early = min(AHEAD, pairs)

    fetch = pltpu.make_async_copy(fields, raw, p_sem.at[0])
    fetch.start()

    me = lax.axis_index("mem")
    here = lax.axis_index("lat")
    count = lax.axis_size("lat")
    parity = lax.rem(here, 2)
    partner = here + 1 - 2 * parity
    hop = 2 - 4 * parity
    target = here + hop
    source = here - hop
    has_target = jnp.logical_and(target >= 0, target < count)
    has_source = jnp.logical_and(source >= 0, source < count)

    barrier = pltpu.get_barrier_semaphore()
    for k in range(1, holders):
        pl.semaphore_signal(
            barrier, inc=1, device_id=(lax.rem(me + k, holders), here), device_id_type=MESH
        )
    pl.semaphore_signal(barrier, inc=1, device_id=(me, partner), device_id_type=MESH)

    @pl.when(has_target)
    def _():
        pl.semaphore_signal(barrier, inc=1, device_id=(me, target), device_id_type=MESH)

    @pl.when(has_source)
    def _():
        pl.semaphore_signal(barrier, inc=1, device_id=(me, source), device_id_type=MESH)

    def gradient_copy(k):
        return pltpu.make_async_remote_copy(
            src_ref=held, dst_ref=gbuf.at[me],
            send_sem=g_send.at[k - 1], recv_sem=g_recv.at[k - 1],
            device_id=(lax.rem(me + k, holders), here), device_id_type=MESH,
        )

    def own_copy(g, holder):
        return pltpu.make_async_remote_copy(
            src_ref=cbuf.at[g, holder], dst_ref=dbuf.at[g, holder],
            send_sem=c_send.at[g, holder], recv_sem=c_recv.at[g, holder],
            device_id=(me, partner), device_id_type=MESH,
        )

    def relay_copy(g, holder):
        return pltpu.make_async_remote_copy(
            src_ref=dbuf.at[g, holder], dst_ref=rbuf.at[g, holder],
            send_sem=f_send.at[g, holder], recv_sem=f_recv.at[g, holder],
            device_id=(me, target), device_id_type=MESH,
        )

    def own_tail(q, holder):
        return pltpu.make_async_remote_copy(
            src_ref=ctail.at[q, holder], dst_ref=dtail.at[q, holder],
            send_sem=ct_send.at[q, holder], recv_sem=ct_recv.at[q, holder],
            device_id=(me, partner), device_id_type=MESH,
        )

    def relay_tail(q, holder):
        return pltpu.make_async_remote_copy(
            src_ref=dtail.at[q, holder], dst_ref=rtail.at[q, holder],
            send_sem=ft_send.at[q, holder], recv_sem=ft_recv.at[q, holder],
            device_id=(me, target), device_id_type=MESH,
        )

    def convert(g, carry=0):
        for slot in range(slots):
            for holder in range(holders):
                pieces = [
                    raw[g * PAIR + i, slot, owner[holder * held_levels + r]].astype(F32)
                    for i in range(PAIR) for r in range(held_levels)
                ]
                pert[g, slot, holder] = jnp.concatenate(pieces, axis=0).astype(BF16)
        return carry

    def place_gradient(holder, block_ref):
        for slot in range(slots):
            pieces = [block_ref[slot, r] for r in range(held_levels)] * PAIR
            grad[slot, holder] = jnp.concatenate(pieces, axis=0)

    def product(g, holder, lanes):
        value = None
        for slot in range(slots):
            term = pert[g, slot, holder, :, lanes].astype(F32) * grad[slot, holder, :, lanes]
            value = term if value is None else value + term
        return value

    def control(g, holder):
        cbuf[g, holder] = product(g, holder, slice(0, main)).astype(BF16)

    place_gradient(me, held)
    fetch.wait()
    convert(0)
    control(0, me)
    pl.semaphore_wait(barrier, holders + has_target.astype(jnp.int32) + has_source.astype(jnp.int32))
    for k in range(1, holders):
        gradient_copy(k).start()
    own_copy(0, me).start()
    for g in range(1, early):
        convert(g)
        control(g, me)
        own_copy(g, me).start()

    @pl.when(jnp.logical_not(has_source))
    def _():
        rbuf[...] = jnp.zeros_like(rbuf)
        rtail[...] = jnp.zeros_like(rtail)

    for k in range(1, holders):
        gradient_copy(k).wait_recv()
        holder = lax.rem(me + holders - k, holders)
        place_gradient(holder, gbuf.at[holder])

    for g in range(early):
        for k in range(1, holders):
            holder = lax.rem(me + k, holders)
            control(g, holder)
            own_copy(g, holder).start()

    total[...] = jnp.zeros_like(total)

    lax.fori_loop(early, pairs, convert, 0)
    for q in range(quads):
        for holder in range(holders):
            tails = [product(q * share + j, holder, slice(main, lon)) for j in range(share)]
            ctail[q, holder] = jnp.concatenate(tails, axis=1).astype(BF16)
            own_tail(q, holder).start()

    def send(g):
        for k in range(holders):
            holder = lax.rem(me + k, holders)
            control(g, holder)
            own_copy(g, holder).start()

    def relay(g):
        for k in range(holders):
            holder = lax.rem(me + k, holders)
            own_copy(g, holder).wait_recv()

            @pl.when(has_target)
            def _():
                relay_copy(g, holder).start()

    def mix(stack):
        mixed = jnp.dot(weights[...], stack, preferred_element_type=F32)
        return mixed[:block] + mixed[block:]

    def mix_tails():
        @pl.when(has_source)
        def _():
            for q in range(quads):
                for holder in range(holders):
                    relay_tail(q, holder).wait_recv()

        for q in range(quads):
            stack = jnp.concatenate(
                [buf[q].reshape(block, LANES) for buf in (ctail, dtail, rtail)], axis=0
            )
            mixed = mix(stack)
            for j in range(share):
                last[q * share + j] = mixed[:, j * rest:(j + 1) * rest]

    def process(g):
        @pl.when(has_source)
        def _():
            for holder in range(holders):
                relay_copy(g, holder).wait_recv()

        stack = jnp.concatenate(
            [buf[g].reshape(block, main) for buf in (cbuf, dbuf, rbuf)], axis=0
        )
        mixed = mix(stack)
        wide[:, :main] = mixed
        tail = last[g]
        wide[:, main:] = jnp.concatenate(
            [tail, mixed[:, :after], mixed[:, main - before:], tail], axis=1
        )
        for holder in range(holders):
            ring = wide[holder * inner:(holder + 1) * inner, :]
            smoothed = rho(0, 3.0) * ring
            for k in range(1, REACH + 1):
                both = pltpu.roll(ring, k, 1) + pltpu.roll(ring, width - k, 1)
                smoothed = smoothed + rho(k, 3.0) * both
            smoothed = smoothed[:, :lon]
            for slot in range(slots):
                total[slot, holder] += pert[g, slot, holder].astype(F32) * smoothed

    def stage(first, last, send_on, relay_on, process_on):
        def step(g, carry):
            if send_on:
                send(g)
            if relay_on:
                relay(g - AHEAD)
            if process_on:
                process(g - AHEAD - LAG)
            return carry

        if first < last:
            lax.fori_loop(first, last, step, 0)

    stage(early, early + 1, True, False, False)
    fill_mixing(weights, owner, holders, held_levels, rows, 1 - 2 * parity)
    relay(0)
    stage(early + 1, 2 * AHEAD, True, True, False)
    for q in range(quads):
        for holder in range(holders):
            own_tail(q, holder).wait_recv()

            @pl.when(has_target)
            def _():
                relay_tail(q, holder).start()

    stage(2 * AHEAD, AHEAD + LAG + 1, True, True, False)
    mix_tails()
    process(0)
    stage(AHEAD + LAG + 1, pairs, True, True, True)
    stage(pairs, pairs + AHEAD, False, True, True)
    stage(pairs + AHEAD, pairs + AHEAD + LAG, False, False, True)

    def total_copy(k):
        return pltpu.make_async_remote_copy(
            src_ref=give.at[k - 1], dst_ref=take.at[k - 1],
            send_sem=t_send.at[k - 1], recv_sem=t_recv.at[k - 1],
            device_id=(lax.rem(me + k, holders), here), device_id_type=MESH,
        )

    for k in range(1, holders):
        holder = lax.rem(me + k, holders)
        for slot in range(slots):
            full = total[slot, holder]
            give[k - 1, slot] = sum(full[i * half:(i + 1) * half] for i in range(1, PAIR)) + full[:half]
        total_copy(k).start()

    for k in range(1, holders):
        gradient_copy(k).wait_send()

    def drain(g, carry):
        for holder in range(holders):
            own_copy(g, holder).wait_send()

            @pl.when(has_target)
            def _():
                relay_copy(g, holder).wait_send()

        return carry

    lax.fori_loop(0, pairs, drain, 0)
    for q in range(quads):
        for holder in range(holders):
            own_tail(q, holder).wait_send()

            @pl.when(has_target)
            def _():
                relay_tail(q, holder).wait_send()

    for k in range(1, holders):
        total_copy(k).wait()
    for slot in range(slots):
        full = total[slot, me]
        value = sum(full[i * half:(i + 1) * half] for i in range(1, PAIR)) + full[:half]
        for k in range(1, holders):
            value = value + take[k - 1, slot]
        for r in range(held_levels):
            out[slot, r] = value[r * rows:(r + 1) * rows]


def local(perturbations, gradient_held, block_owner):
    members, slots, levels, rows, lon = perturbations.shape
    held_levels = gradient_held.shape[1]
    holders = levels // held_levels
    pairs = members // PAIR
    inner = PAIR * held_levels * rows
    block = holders * inner
    others = max(holders - 1, 1)
    width = -(-(lon + 2 * REACH) // LANES) * LANES
    main = lon // LANES * LANES
    rest = lon - main
    share = LANES // rest
    quads = pairs // share
    part = (slots, held_levels, rows, lon)
    dma = pltpu.SemaphoreType.DMA
    return pl.pallas_call(
        kernel,
        out_shape=jax.ShapeDtypeStruct(part, F32),
        in_specs=[
            pl.BlockSpec(memory_space=pltpu.SMEM),
            pl.BlockSpec(memory_space=pltpu.HBM),
            pl.BlockSpec(memory_space=pltpu.VMEM),
        ],
        out_specs=pl.BlockSpec(memory_space=pltpu.VMEM),
        scratch_shapes=[
            pltpu.VMEM((members, slots, levels, rows, lon), BF16),
            pltpu.VMEM((pairs, slots, holders, inner, lon), BF16),
            pltpu.VMEM((holders,) + part, F32),
            pltpu.VMEM((slots, holders, inner, lon), F32),
            pltpu.VMEM((pairs, holders, inner, main), BF16),
            pltpu.VMEM((pairs, holders, inner, main), BF16),
            pltpu.VMEM((pairs, holders, inner, main), BF16),
            pltpu.VMEM((quads, holders, inner, LANES), BF16),
            pltpu.VMEM((quads, holders, inner, LANES), BF16),
            pltpu.VMEM((quads, holders, inner, LANES), BF16),
            pltpu.VMEM((2 * block, 3 * block), BF16),
            pltpu.VMEM((pairs, block, rest), F32),
            pltpu.VMEM((block, width), F32),
            pltpu.VMEM((slots, holders, inner, lon), F32),
            pltpu.VMEM((others, slots, held_levels * rows, lon), F32),
            pltpu.VMEM((others, slots, held_levels * rows, lon), F32),
            dma((1,)),
            dma((others,)), dma((others,)),
            dma((pairs, holders)), dma((pairs, holders)),
            dma((pairs, holders)), dma((pairs, holders)),
            dma((quads, holders)), dma((quads, holders)),
            dma((quads, holders)), dma((quads, holders)),
            dma((others,)), dma((others,)),
        ],
        compiler_params=pltpu.CompilerParams(
            collective_id=0, has_side_effects=True, vmem_limit_bytes=538 * 1024 * 1024 // 10
        ),
    )(block_owner, perturbations, gradient_held)


def solution(mesh):
    placed = (P("mem", None, None, "lat", None), P(None, "mem", "lat", None), P())
    return jax.shard_map(
        local, mesh=mesh, in_specs=placed, out_specs=P(None, "mem", "lat", None), check_vma=False,
    )
```

```python
import functools
import math

import jax
import jax.numpy as jnp
from jax import lax
from jax.experimental import pallas as pl
from jax.experimental.pallas import tpu as pltpu
from jax.sharding import PartitionSpec as P

MESH = pl.DeviceIdType.MESH
REACH = 4
LANES = 128
PAIR = 2
AHEAD = 2
LAG = 3
F32 = jnp.float32
BF16 = jnp.bfloat16


def rho(offset, spread):
    return math.exp(-(offset * offset) / (2.0 * spread * spread))


def rho_of(apart, spread):
    value = jnp.zeros(apart.shape, F32)
    for a in range(REACH + 1):
        value = jnp.where(jnp.abs(apart) == a, rho(a, spread), value)
    return value


def fill_mixing(weights, owner, holders, held_levels, rows, direct):
    inner = PAIR * held_levels * rows
    block = holders * inner

    def places(axis):
        index = lax.broadcasted_iota(jnp.int32, (block, 3 * block), axis)
        part = jnp.where(index >= block, 1, 0) + jnp.where(index >= 2 * block, 1, 0)
        index = index - part * block
        level = jnp.zeros_like(index)
        member = jnp.zeros_like(index)
        row = index
        for p in range(holders * held_levels):
            for i in range(PAIR):
                start = (p // held_levels) * inner + (i * held_levels + p % held_levels) * rows
                inside = jnp.logical_and(index >= start, index < start + rows)
                level = jnp.where(inside, owner[p], level)
                member = jnp.where(inside, i, member)
                row = jnp.where(inside, index - start, row)
        shift = jnp.where(part == 1, direct, jnp.where(part == 2, -direct, 0))
        return level, member, row + shift * rows

    to_level, to_member, to_row = places(0)
    from_level, from_member, from_row = places(1)
    exact = rho_of(from_level - to_level, 2.0) * rho_of(from_row - to_row, 2.5)
    exact = jnp.where(from_member == to_member, exact, 0.0)
    high = exact.astype(BF16)
    weights[:block, :] = high
    weights[block:, :] = (exact - high.astype(F32)).astype(BF16)


def kernel(
    owner, fields, held_far, out,
    raw, raw_first, held, pert, gbuf, grad, cbuf, dbuf, rbuf, ctail, dtail, rtail, weights, last, wide, total, give, take,
    p_sem, g_send, g_recv, c_send, c_recv, f_send, f_recv,
    ct_send, ct_recv, ft_send, ft_recv, t_send, t_recv,
):
    members, slots, levels, rows, lon = fields.shape
    held_levels = held.shape[1]
    holders = levels // held_levels
    pairs = members // PAIR
    inner = PAIR * held_levels * rows
    block = holders * inner
    half = held_levels * rows
    width = wide.shape[1]
    main = cbuf.shape[-1]
    rest = lon - main
    share = LANES // rest
    quads = pairs // share
    after = (width - lon) // 2
    before = width - lon - after - rest
    early = min(AHEAD, pairs)

    first_fetch = pltpu.make_async_copy(fields.at[pl.ds(0, PAIR)], raw_first, p_sem.at[0])
    held_fetch = pltpu.make_async_copy(held_far, held, p_sem.at[1])
    fetch = pltpu.make_async_copy(fields.at[pl.ds(PAIR, members - PAIR)], raw, p_sem.at[2])

    me = lax.axis_index("mem")
    here = lax.axis_index("lat")
    count = lax.axis_size("lat")
    parity = lax.rem(here, 2)
    partner = here + 1 - 2 * parity
    hop = 2 - 4 * parity
    target = here + hop
    source = here - hop
    has_target = jnp.logical_and(target >= 0, target < count)
    has_source = jnp.logical_and(source >= 0, source < count)

    barrier = pltpu.get_barrier_semaphore()
    for k in range(1, holders):
        pl.semaphore_signal(
            barrier, inc=1, device_id=(lax.rem(me + k, holders), here), device_id_type=MESH
        )
    pl.semaphore_signal(barrier, inc=1, device_id=(me, partner), device_id_type=MESH)

    @pl.when(has_target)
    def _():
        pl.semaphore_signal(barrier, inc=1, device_id=(me, target), device_id_type=MESH)

    @pl.when(has_source)
    def _():
        pl.semaphore_signal(barrier, inc=1, device_id=(me, source), device_id_type=MESH)

    held_fetch.start()
    first_fetch.start()
    fetch.start()

    def gradient_copy(k):
        return pltpu.make_async_remote_copy(
            src_ref=held, dst_ref=gbuf.at[me],
            send_sem=g_send.at[k - 1], recv_sem=g_recv.at[k - 1],
            device_id=(lax.rem(me + k, holders), here), device_id_type=MESH,
        )

    def own_copy(g, holder):
        return pltpu.make_async_remote_copy(
            src_ref=cbuf.at[g, holder], dst_ref=dbuf.at[g, holder],
            send_sem=c_send.at[g, holder], recv_sem=c_recv.at[g, holder],
            device_id=(me, partner), device_id_type=MESH,
        )

    def relay_copy(g, holder):
        return pltpu.make_async_remote_copy(
            src_ref=dbuf.at[g, holder], dst_ref=rbuf.at[g, holder],
            send_sem=f_send.at[g, holder], recv_sem=f_recv.at[g, holder],
            device_id=(me, target), device_id_type=MESH,
        )

    def own_tail(q, holder):
        return pltpu.make_async_remote_copy(
            src_ref=ctail.at[q, holder], dst_ref=dtail.at[q, holder],
            send_sem=ct_send.at[q, holder], recv_sem=ct_recv.at[q, holder],
            device_id=(me, partner), device_id_type=MESH,
        )

    def relay_tail(q, holder):
        return pltpu.make_async_remote_copy(
            src_ref=dtail.at[q, holder], dst_ref=rtail.at[q, holder],
            send_sem=ft_send.at[q, holder], recv_sem=ft_recv.at[q, holder],
            device_id=(me, target), device_id_type=MESH,
        )

    def convert_from(source, first, g):
        for slot in range(slots):
            for holder in range(holders):
                pieces = [
                    source[first + i, slot, owner[holder * held_levels + r]].astype(F32)
                    for i in range(PAIR) for r in range(held_levels)
                ]
                pert[g, slot, holder] = jnp.concatenate(pieces, axis=0).astype(BF16)

    def convert(g, carry=0):
        convert_from(raw, (g - 1) * PAIR, g)
        return carry

    def place_gradient(holder, block_ref):
        for slot in range(slots):
            pieces = [block_ref[slot, r] for r in range(held_levels)] * PAIR
            grad[slot, holder] = jnp.concatenate(pieces, axis=0)

    def product(g, holder, lanes):
        value = None
        for slot in range(slots):
            term = pert[g, slot, holder, :, lanes].astype(F32) * grad[slot, holder, :, lanes]
            value = term if value is None else value + term
        return value

    def control(g, holder):
        cbuf[g, holder] = product(g, holder, slice(0, main)).astype(BF16)

    held_fetch.wait()
    place_gradient(me, held)
    first_fetch.wait()
    convert_from(raw_first, 0, 0)
    control(0, me)
    pl.semaphore_wait(barrier, holders + has_target.astype(jnp.int32) + has_source.astype(jnp.int32))
    for k in range(1, holders):
        gradient_copy(k).start()
    own_copy(0, me).start()
    fetch.wait()
    for g in range(1, early):
        convert(g)
        control(g, me)
        own_copy(g, me).start()

    @pl.when(jnp.logical_not(has_source))
    def _():
        rbuf[...] = jnp.zeros_like(rbuf)
        rtail[...] = jnp.zeros_like(rtail)

    for k in range(1, holders):
        gradient_copy(k).wait_recv()
        holder = lax.rem(me + holders - k, holders)
        place_gradient(holder, gbuf.at[holder])

    for g in range(early):
        for k in range(1, holders):
            holder = lax.rem(me + k, holders)
            control(g, holder)
            own_copy(g, holder).start()

    total[...] = jnp.zeros_like(total)

    lax.fori_loop(early, pairs, convert, 0)
    for q in range(quads):
        for holder in range(holders):
            tails = [product(q * share + j, holder, slice(main, lon)) for j in range(share)]
            ctail[q, holder] = jnp.concatenate(tails, axis=1).astype(BF16)
            own_tail(q, holder).start()

    def send(g):
        for k in range(holders):
            holder = lax.rem(me + k, holders)
            control(g, holder)
            own_copy(g, holder).start()

    def relay(g):
        for k in range(holders):
            holder = lax.rem(me + k, holders)
            own_copy(g, holder).wait_recv()

            @pl.when(has_target)
            def _():
                relay_copy(g, holder).start()

    def mix(stack):
        mixed = jnp.dot(weights[...], stack, preferred_element_type=F32)
        return mixed[:block] + mixed[block:]

    def mix_tails():
        @pl.when(has_source)
        def _():
            for q in range(quads):
                for holder in range(holders):
                    relay_tail(q, holder).wait_recv()

        for q in range(quads):
            stack = jnp.concatenate(
                [buf[q].reshape(block, LANES) for buf in (ctail, dtail, rtail)], axis=0
            )
            mixed = mix(stack)
            for j in range(share):
                last[q * share + j] = mixed[:, j * rest:(j + 1) * rest]

    def process(g):
        @pl.when(has_source)
        def _():
            for holder in range(holders):
                relay_copy(g, holder).wait_recv()

        stack = jnp.concatenate(
            [buf[g].reshape(block, main) for buf in (cbuf, dbuf, rbuf)], axis=0
        )
        mixed = mix(stack)
        wide[:, :main] = mixed
        tail = last[g]
        wide[:, main:] = jnp.concatenate(
            [tail, mixed[:, :after], mixed[:, main - before:], tail], axis=1
        )
        for holder in range(holders):
            ring = wide[holder * inner:(holder + 1) * inner, :]
            smoothed = rho(0, 3.0) * ring
            for k in range(1, REACH + 1):
                both = pltpu.roll(ring, k, 1) + pltpu.roll(ring, width - k, 1)
                smoothed = smoothed + rho(k, 3.0) * both
            smoothed = smoothed[:, :lon]
            for slot in range(slots):
                total[slot, holder] += pert[g, slot, holder].astype(F32) * smoothed

    def stage(first, last, send_on, relay_on, process_on):
        def step(g, carry):
            if send_on:
                send(g)
            if relay_on:
                relay(g - AHEAD)
            if process_on:
                process(g - AHEAD - LAG)
            return carry

        if first < last:
            lax.fori_loop(first, last, step, 0)

    stage(early, early + 1, True, False, False)
    fill_mixing(weights, owner, holders, held_levels, rows, 1 - 2 * parity)
    relay(0)
    stage(early + 1, 2 * AHEAD, True, True, False)
    for q in range(quads):
        for holder in range(holders):
            own_tail(q, holder).wait_recv()

            @pl.when(has_target)
            def _():
                relay_tail(q, holder).start()

    stage(2 * AHEAD, AHEAD + LAG + 1, True, True, False)
    mix_tails()
    process(0)
    stage(AHEAD + LAG + 1, pairs, True, True, True)
    stage(pairs, pairs + AHEAD, False, True, True)
    stage(pairs + AHEAD, pairs + AHEAD + LAG, False, False, True)

    def total_copy(k):
        return pltpu.make_async_remote_copy(
            src_ref=give.at[k - 1], dst_ref=take.at[k - 1],
            send_sem=t_send.at[k - 1], recv_sem=t_recv.at[k - 1],
            device_id=(lax.rem(me + k, holders), here), device_id_type=MESH,
        )

    for k in range(1, holders):
        holder = lax.rem(me + k, holders)
        for slot in range(slots):
            full = total[slot, holder]
            give[k - 1, slot] = sum(full[i * half:(i + 1) * half] for i in range(1, PAIR)) + full[:half]
        total_copy(k).start()

    for k in range(1, holders):
        gradient_copy(k).wait_send()

    def drain(g, carry):
        for holder in range(holders):
            own_copy(g, holder).wait_send()

            @pl.when(has_target)
            def _():
                relay_copy(g, holder).wait_send()

        return carry

    lax.fori_loop(0, pairs, drain, 0)
    for q in range(quads):
        for holder in range(holders):
            own_tail(q, holder).wait_send()

            @pl.when(has_target)
            def _():
                relay_tail(q, holder).wait_send()

    for k in range(1, holders):
        total_copy(k).wait()
    for slot in range(slots):
        full = total[slot, me]
        value = sum(full[i * half:(i + 1) * half] for i in range(1, PAIR)) + full[:half]
        for k in range(1, holders):
            value = value + take[k - 1, slot]
        for r in range(held_levels):
            out[slot, r] = value[r * rows:(r + 1) * rows]


def local(perturbations, gradient_held, block_owner):
    members, slots, levels, rows, lon = perturbations.shape
    held_levels = gradient_held.shape[1]
    holders = levels // held_levels
    pairs = members // PAIR
    inner = PAIR * held_levels * rows
    block = holders * inner
    others = max(holders - 1, 1)
    width = -(-(lon + 2 * REACH) // LANES) * LANES
    main = lon // LANES * LANES
    rest = lon - main
    share = LANES // rest
    quads = pairs // share
    part = (slots, held_levels, rows, lon)
    dma = pltpu.SemaphoreType.DMA
    return pl.pallas_call(
        kernel,
        out_shape=jax.ShapeDtypeStruct(part, F32),
        in_specs=[
            pl.BlockSpec(memory_space=pltpu.SMEM),
            pl.BlockSpec(memory_space=pltpu.HBM),
            pl.BlockSpec(memory_space=pltpu.HBM),
        ],
        out_specs=pl.BlockSpec(memory_space=pltpu.VMEM),
        scratch_shapes=[
            pltpu.VMEM((members - PAIR, slots, levels, rows, lon), BF16),
            pltpu.VMEM((PAIR, slots, levels, rows, lon), BF16),
            pltpu.VMEM(part, F32),
            pltpu.VMEM((pairs, slots, holders, inner, lon), BF16),
            pltpu.VMEM((holders,) + part, F32),
            pltpu.VMEM((slots, holders, inner, lon), F32),
            pltpu.VMEM((pairs, holders, inner, main), BF16),
            pltpu.VMEM((pairs, holders, inner, main), BF16),
            pltpu.VMEM((pairs, holders, inner, main), BF16),
            pltpu.VMEM((quads, holders, inner, LANES), BF16),
            pltpu.VMEM((quads, holders, inner, LANES), BF16),
            pltpu.VMEM((quads, holders, inner, LANES), BF16),
            pltpu.VMEM((2 * block, 3 * block), BF16),
            pltpu.VMEM((pairs, block, rest), F32),
            pltpu.VMEM((block, width), F32),
            pltpu.VMEM((slots, holders, inner, lon), F32),
            pltpu.VMEM((others, slots, held_levels * rows, lon), F32),
            pltpu.VMEM((others, slots, held_levels * rows, lon), F32),
            dma((3,)),
            dma((others,)), dma((others,)),
            dma((pairs, holders)), dma((pairs, holders)),
            dma((pairs, holders)), dma((pairs, holders)),
            dma((quads, holders)), dma((quads, holders)),
            dma((quads, holders)), dma((quads, holders)),
            dma((others,)), dma((others,)),
        ],
        compiler_params=pltpu.CompilerParams(
            collective_id=0, has_side_effects=True, vmem_limit_bytes=538 * 1024 * 1024 // 10
        ),
    )(block_owner, perturbations, gradient_held)


def solution(mesh):
    placed = (P("mem", None, None, "lat", None), P(None, "mem", "lat", None), P())
    return jax.shard_map(
        local, mesh=mesh, in_specs=placed, out_specs=P(None, "mem", "lat", None), check_vma=False,
    )
```

```python
import functools
import math

import jax
import jax.numpy as jnp
from jax import lax
from jax.experimental import pallas as pl
from jax.experimental.pallas import tpu as pltpu
from jax.sharding import PartitionSpec as P

MESH = pl.DeviceIdType.MESH
REACH = 4
LANES = 128
PAIR = 2
AHEAD = 2
LAG = 3
F32 = jnp.float32
BF16 = jnp.bfloat16


def rho(offset, spread):
    return math.exp(-(offset * offset) / (2.0 * spread * spread))


def rho_of(apart, spread):
    value = jnp.zeros(apart.shape, F32)
    for a in range(REACH + 1):
        value = jnp.where(jnp.abs(apart) == a, rho(a, spread), value)
    return value


def fill_mixing(weights, owner, holders, held_levels, rows, direct):
    inner = PAIR * held_levels * rows
    block = holders * inner

    def places(axis):
        index = lax.broadcasted_iota(jnp.int32, (block, 3 * block), axis)
        part = jnp.where(index >= block, 1, 0) + jnp.where(index >= 2 * block, 1, 0)
        index = index - part * block
        level = jnp.zeros_like(index)
        member = jnp.zeros_like(index)
        row = index
        for p in range(holders * held_levels):
            for i in range(PAIR):
                start = (p // held_levels) * inner + (i * held_levels + p % held_levels) * rows
                inside = jnp.logical_and(index >= start, index < start + rows)
                level = jnp.where(inside, owner[p], level)
                member = jnp.where(inside, i, member)
                row = jnp.where(inside, index - start, row)
        shift = jnp.where(part == 1, direct, jnp.where(part == 2, -direct, 0))
        return level, member, row + shift * rows

    to_level, to_member, to_row = places(0)
    from_level, from_member, from_row = places(1)
    exact = rho_of(from_level - to_level, 2.0) * rho_of(from_row - to_row, 2.5)
    exact = jnp.where(from_member == to_member, exact, 0.0)
    high = exact.astype(BF16)
    weights[:block, :] = high
    weights[block:, :] = (exact - high.astype(F32)).astype(BF16)


def kernel(
    owner, fields, held_far, out,
    raw, raw_first, held, pert, gbuf, grad, cbuf, dbuf, rbuf, ctail, dtail, rtail, weights, last, wide, total, give, take,
    p_sem, g_send, g_recv, c_send, c_recv, f_send, f_recv,
    ct_send, ct_recv, ft_send, ft_recv, t_send, t_recv,
):
    members, slots, levels, rows, lon = fields.shape
    held_levels = held.shape[1]
    holders = levels // held_levels
    pairs = members // PAIR
    inner = PAIR * held_levels * rows
    block = holders * inner
    half = held_levels * rows
    width = wide.shape[1]
    main = cbuf.shape[-1]
    rest = lon - main
    share = LANES // rest
    quads = pairs // share
    after = (width - lon) // 2
    before = width - lon - after - rest
    early = min(AHEAD, pairs)

    first_fetch = pltpu.make_async_copy(fields.at[pl.ds(0, PAIR)], raw_first, p_sem.at[0])
    held_fetch = pltpu.make_async_copy(held_far, held, p_sem.at[1])
    fetch = pltpu.make_async_copy(fields.at[pl.ds(PAIR, members - PAIR)], raw, p_sem.at[2])

    me = lax.axis_index("mem")
    here = lax.axis_index("lat")
    count = lax.axis_size("lat")
    parity = lax.rem(here, 2)
    partner = here + 1 - 2 * parity
    hop = 2 - 4 * parity
    target = here + hop
    source = here - hop
    has_target = jnp.logical_and(target >= 0, target < count)
    has_source = jnp.logical_and(source >= 0, source < count)

    barrier = pltpu.get_barrier_semaphore()
    for k in range(1, holders):
        pl.semaphore_signal(
            barrier, inc=1, device_id=(lax.rem(me + k, holders), here), device_id_type=MESH
        )
    pl.semaphore_signal(barrier, inc=1, device_id=(me, partner), device_id_type=MESH)

    @pl.when(has_target)
    def _():
        pl.semaphore_signal(barrier, inc=1, device_id=(me, target), device_id_type=MESH)

    @pl.when(has_source)
    def _():
        pl.semaphore_signal(barrier, inc=1, device_id=(me, source), device_id_type=MESH)

    held_fetch.start()
    first_fetch.start()
    fetch.start()

    def gradient_copy(k):
        return pltpu.make_async_remote_copy(
            src_ref=held, dst_ref=gbuf.at[me],
            send_sem=g_send.at[k - 1], recv_sem=g_recv.at[k - 1],
            device_id=(lax.rem(me + k, holders), here), device_id_type=MESH,
        )

    def own_copy(g, holder):
        return pltpu.make_async_remote_copy(
            src_ref=cbuf.at[g, holder], dst_ref=dbuf.at[g, holder],
            send_sem=c_send.at[g, holder], recv_sem=c_recv.at[g, holder],
            device_id=(me, partner), device_id_type=MESH,
        )

    def relay_copy(g, holder):
        return pltpu.make_async_remote_copy(
            src_ref=dbuf.at[g, holder], dst_ref=rbuf.at[g, holder],
            send_sem=f_send.at[g, holder], recv_sem=f_recv.at[g, holder],
            device_id=(me, target), device_id_type=MESH,
        )

    def own_tail(q, holder):
        return pltpu.make_async_remote_copy(
            src_ref=ctail.at[q, holder], dst_ref=dtail.at[q, holder],
            send_sem=ct_send.at[q, holder], recv_sem=ct_recv.at[q, holder],
            device_id=(me, partner), device_id_type=MESH,
        )

    def relay_tail(q, holder):
        return pltpu.make_async_remote_copy(
            src_ref=dtail.at[q, holder], dst_ref=rtail.at[q, holder],
            send_sem=ft_send.at[q, holder], recv_sem=ft_recv.at[q, holder],
            device_id=(me, target), device_id_type=MESH,
        )

    def convert_from(source, first, g):
        for slot in range(slots):
            for holder in range(holders):
                pieces = [
                    source[first + i, slot, owner[holder * held_levels + r]].astype(F32)
                    for i in range(PAIR) for r in range(held_levels)
                ]
                pert[g, slot, holder] = jnp.concatenate(pieces, axis=0).astype(BF16)

    def convert(g, carry=0):
        convert_from(raw, (g - 1) * PAIR, g)
        return carry

    def place_gradient(holder, block_ref):
        for slot in range(slots):
            pieces = [block_ref[slot, r] for r in range(held_levels)] * PAIR
            grad[slot, holder] = jnp.concatenate(pieces, axis=0)

    def product(g, holder, lanes):
        value = None
        for slot in range(slots):
            term = pert[g, slot, holder, :, lanes].astype(F32) * grad[slot, holder, :, lanes]
            value = term if value is None else value + term
        return value

    def control(g, holder):
        cbuf[g, holder] = product(g, holder, slice(0, main)).astype(BF16)

    held_fetch.wait()
    place_gradient(me, held)
    first_fetch.wait()
    convert_from(raw_first, 0, 0)
    control(0, me)
    pl.semaphore_wait(barrier, holders + has_target.astype(jnp.int32) + has_source.astype(jnp.int32))
    for k in range(1, holders):
        gradient_copy(k).start()
    own_copy(0, me).start()
    fetch.wait()
    for g in range(1, early):
        convert(g)
        control(g, me)
        own_copy(g, me).start()

    @pl.when(jnp.logical_not(has_source))
    def _():
        rbuf[...] = jnp.zeros_like(rbuf)
        rtail[...] = jnp.zeros_like(rtail)

    for k in range(1, holders):
        gradient_copy(k).wait_recv()
        holder = lax.rem(me + holders - k, holders)
        place_gradient(holder, gbuf.at[holder])

    for g in range(early):
        for k in range(1, holders):
            holder = lax.rem(me + k, holders)
            control(g, holder)
            own_copy(g, holder).start()

    def send_tails(q):
        for holder in range(holders):
            tails = [product(q * share + j, holder, slice(main, lon)) for j in range(share)]
            ctail[q, holder] = jnp.concatenate(tails, axis=1).astype(BF16)
            own_tail(q, holder).start()

    def pass_tails(q):
        for holder in range(holders):
            own_tail(q, holder).wait_recv()

            @pl.when(has_target)
            def _():
                relay_tail(q, holder).start()

    def send(g):
        for k in range(holders):
            holder = lax.rem(me + k, holders)
            control(g, holder)
            own_copy(g, holder).start()

    def relay_one(g, holder):
        own_copy(g, holder).wait_recv()

        @pl.when(has_target)
        def _():
            relay_copy(g, holder).start()

    def relay(g, first=0):
        for k in range(first, holders):
            relay_one(g, lax.rem(me + k, holders))

    def mix(stack):
        mixed = jnp.dot(weights[...], stack, preferred_element_type=F32)
        return mixed[:block] + mixed[block:]

    def mix_tails(q):
        @pl.when(has_source)
        def _():
            for holder in range(holders):
                relay_tail(q, holder).wait_recv()

        stack = jnp.concatenate(
            [buf[q].reshape(block, LANES) for buf in (ctail, dtail, rtail)], axis=0
        )
        mixed = mix(stack)
        for j in range(share):
            last[q * share + j] = mixed[:, j * rest:(j + 1) * rest]

    def process(g):
        @pl.when(has_source)
        def _():
            for holder in range(holders):
                relay_copy(g, holder).wait_recv()

        stack = jnp.concatenate(
            [buf[g].reshape(block, main) for buf in (cbuf, dbuf, rbuf)], axis=0
        )
        mixed = mix(stack)
        wide[:, :main] = mixed
        tail = last[g]
        wide[:, main:] = jnp.concatenate(
            [tail, mixed[:, :after], mixed[:, main - before:], tail], axis=1
        )
        for holder in range(holders):
            ring = wide[holder * inner:(holder + 1) * inner, :]
            smoothed = rho(0, 3.0) * ring
            for k in range(1, REACH + 1):
                both = pltpu.roll(ring, k, 1) + pltpu.roll(ring, width - k, 1)
                smoothed = smoothed + rho(k, 3.0) * both
            smoothed = smoothed[:, :lon]
            for slot in range(slots):
                total[slot, holder] += pert[g, slot, holder].astype(F32) * smoothed

    def stage(first, last, send_on, relay_on, process_on):
        def step(g, carry):
            if send_on:
                send(g)
            if relay_on:
                relay(g - AHEAD)
            if process_on:
                process(g - AHEAD - LAG)
            return carry

        if first < last:
            lax.fori_loop(first, last, step, 0)

    relay_one(0, me)
    convert(early)
    send(early)
    relay_one(1, me)
    convert(early + 1)
    relay(0, 1)
    send_tails(0)
    send(early + 1)
    relay(1, 1)
    total[...] = jnp.zeros_like(total)
    fill_mixing(weights, owner, holders, held_levels, rows, 1 - 2 * parity)
    lax.fori_loop(early + 2, pairs, convert, 0)
    for q in range(1, quads):
        send_tails(q)
    stage(2 * AHEAD, 2 * AHEAD + 1, True, True, False)
    pass_tails(0)
    stage(2 * AHEAD + 1, AHEAD + LAG + 1, True, True, False)
    for q in range(1, quads):
        pass_tails(q)
    mix_tails(0)
    process(0)
    stage(AHEAD + LAG + 1, pairs, True, True, True)
    for q in range(1, quads):
        mix_tails(q)
    stage(pairs, pairs + AHEAD, False, True, True)
    stage(pairs + AHEAD, pairs + AHEAD + LAG, False, False, True)

    def total_copy(k):
        return pltpu.make_async_remote_copy(
            src_ref=give.at[k - 1], dst_ref=take.at[k - 1],
            send_sem=t_send.at[k - 1], recv_sem=t_recv.at[k - 1],
            device_id=(lax.rem(me + k, holders), here), device_id_type=MESH,
        )

    for k in range(1, holders):
        holder = lax.rem(me + k, holders)
        for slot in range(slots):
            full = total[slot, holder]
            give[k - 1, slot] = sum(full[i * half:(i + 1) * half] for i in range(1, PAIR)) + full[:half]
        total_copy(k).start()

    for k in range(1, holders):
        gradient_copy(k).wait_send()

    def drain(g, carry):
        for holder in range(holders):
            own_copy(g, holder).wait_send()

            @pl.when(has_target)
            def _():
                relay_copy(g, holder).wait_send()

        return carry

    lax.fori_loop(0, pairs, drain, 0)
    for q in range(quads):
        for holder in range(holders):
            own_tail(q, holder).wait_send()

            @pl.when(has_target)
            def _():
                relay_tail(q, holder).wait_send()

    for k in range(1, holders):
        total_copy(k).wait()
    for slot in range(slots):
        full = total[slot, me]
        value = sum(full[i * half:(i + 1) * half] for i in range(1, PAIR)) + full[:half]
        for k in range(1, holders):
            value = value + take[k - 1, slot]
        for r in range(held_levels):
            out[slot, r] = value[r * rows:(r + 1) * rows]


def local(perturbations, gradient_held, block_owner):
    members, slots, levels, rows, lon = perturbations.shape
    held_levels = gradient_held.shape[1]
    holders = levels // held_levels
    pairs = members // PAIR
    inner = PAIR * held_levels * rows
    block = holders * inner
    others = max(holders - 1, 1)
    width = -(-(lon + 2 * REACH) // LANES) * LANES
    main = lon // LANES * LANES
    rest = lon - main
    share = LANES // rest
    quads = pairs // share
    part = (slots, held_levels, rows, lon)
    dma = pltpu.SemaphoreType.DMA
    return pl.pallas_call(
        kernel,
        out_shape=jax.ShapeDtypeStruct(part, F32),
        in_specs=[
            pl.BlockSpec(memory_space=pltpu.SMEM),
            pl.BlockSpec(memory_space=pltpu.HBM),
            pl.BlockSpec(memory_space=pltpu.HBM),
        ],
        out_specs=pl.BlockSpec(memory_space=pltpu.VMEM),
        scratch_shapes=[
            pltpu.VMEM((members - PAIR, slots, levels, rows, lon), BF16),
            pltpu.VMEM((PAIR, slots, levels, rows, lon), BF16),
            pltpu.VMEM(part, F32),
            pltpu.VMEM((pairs, slots, holders, inner, lon), BF16),
            pltpu.VMEM((holders,) + part, F32),
            pltpu.VMEM((slots, holders, inner, lon), F32),
            pltpu.VMEM((pairs, holders, inner, main), BF16),
            pltpu.VMEM((pairs, holders, inner, main), BF16),
            pltpu.VMEM((pairs, holders, inner, main), BF16),
            pltpu.VMEM((quads, holders, inner, LANES), BF16),
            pltpu.VMEM((quads, holders, inner, LANES), BF16),
            pltpu.VMEM((quads, holders, inner, LANES), BF16),
            pltpu.VMEM((2 * block, 3 * block), BF16),
            pltpu.VMEM((pairs, block, rest), F32),
            pltpu.VMEM((block, width), F32),
            pltpu.VMEM((slots, holders, inner, lon), F32),
            pltpu.VMEM((others, slots, held_levels * rows, lon), F32),
            pltpu.VMEM((others, slots, held_levels * rows, lon), F32),
            dma((3,)),
            dma((others,)), dma((others,)),
            dma((pairs, holders)), dma((pairs, holders)),
            dma((pairs, holders)), dma((pairs, holders)),
            dma((quads, holders)), dma((quads, holders)),
            dma((quads, holders)), dma((quads, holders)),
            dma((others,)), dma((others,)),
        ],
        compiler_params=pltpu.CompilerParams(
            collective_id=0, has_side_effects=True, vmem_limit_bytes=538 * 1024 * 1024 // 10
        ),
    )(block_owner, perturbations, gradient_held)


def solution(mesh):
    placed = (P("mem", None, None, "lat", None), P(None, "mem", "lat", None), P())
    return jax.shard_map(
        local, mesh=mesh, in_specs=placed, out_specs=P(None, "mem", "lat", None), check_vma=False,
    )
```

```python
import functools
import math

import jax
import jax.numpy as jnp
from jax import lax
from jax.experimental import pallas as pl
from jax.experimental.pallas import tpu as pltpu
from jax.sharding import PartitionSpec as P

MESH = pl.DeviceIdType.MESH
REACH = 4
LANES = 128
PAIR = 2
AHEAD = 2
LAG = 4
F32 = jnp.float32
BF16 = jnp.bfloat16


def rho(offset, spread):
    return math.exp(-(offset * offset) / (2.0 * spread * spread))


def rho_of(apart, spread):
    value = jnp.zeros(apart.shape, F32)
    for a in range(REACH + 1):
        value = jnp.where(jnp.abs(apart) == a, rho(a, spread), value)
    return value


def fill_mixing(weights, owner, holders, held_levels, rows, direct):
    inner = PAIR * held_levels * rows
    block = holders * inner

    def places(axis):
        index = lax.broadcasted_iota(jnp.int32, (block, 3 * block), axis)
        part = jnp.where(index >= block, 1, 0) + jnp.where(index >= 2 * block, 1, 0)
        index = index - part * block
        level = jnp.zeros_like(index)
        member = jnp.zeros_like(index)
        row = index
        for p in range(holders * held_levels):
            for i in range(PAIR):
                start = (p // held_levels) * inner + (i * held_levels + p % held_levels) * rows
                inside = jnp.logical_and(index >= start, index < start + rows)
                level = jnp.where(inside, owner[p], level)
                member = jnp.where(inside, i, member)
                row = jnp.where(inside, index - start, row)
        shift = jnp.where(part == 1, direct, jnp.where(part == 2, -direct, 0))
        return level, member, row + shift * rows

    to_level, to_member, to_row = places(0)
    from_level, from_member, from_row = places(1)
    exact = rho_of(from_level - to_level, 2.0) * rho_of(from_row - to_row, 2.5)
    exact = jnp.where(from_member == to_member, exact, 0.0)
    high = exact.astype(BF16)
    weights[:block, :] = high
    weights[block:, :] = (exact - high.astype(F32)).astype(BF16)


def kernel(
    owner, fields, held_far, out,
    raw, raw_first, held, pert, gbuf, grad, cbuf, dbuf, rbuf, ctail, dtail, rtail, weights, last, wide, total, give, take,
    p_sem, g_send, g_recv, c_send, c_recv, f_send, f_recv,
    ct_send, ct_recv, ft_send, ft_recv, t_send, t_recv,
):
    members, slots, levels, rows, lon = fields.shape
    held_levels = held.shape[1]
    holders = levels // held_levels
    pairs = members // PAIR
    inner = PAIR * held_levels * rows
    block = holders * inner
    half = held_levels * rows
    width = wide.shape[1]
    main = cbuf.shape[-1]
    rest = lon - main
    share = LANES // rest
    quads = pairs // share
    after = (width - lon) // 2
    before = width - lon - after - rest
    early = min(AHEAD, pairs)

    first_fetch = pltpu.make_async_copy(fields.at[pl.ds(0, PAIR)], raw_first, p_sem.at[0])
    held_fetch = pltpu.make_async_copy(held_far, held, p_sem.at[1])
    fetch = pltpu.make_async_copy(fields.at[pl.ds(PAIR, members - PAIR)], raw, p_sem.at[2])

    me = lax.axis_index("mem")
    here = lax.axis_index("lat")
    count = lax.axis_size("lat")
    parity = lax.rem(here, 2)
    partner = here + 1 - 2 * parity
    hop = 2 - 4 * parity
    target = here + hop
    source = here - hop
    has_target = jnp.logical_and(target >= 0, target < count)
    has_source = jnp.logical_and(source >= 0, source < count)

    barrier = pltpu.get_barrier_semaphore()
    for k in range(1, holders):
        pl.semaphore_signal(
            barrier, inc=1, device_id=(lax.rem(me + k, holders), here), device_id_type=MESH
        )
    pl.semaphore_signal(barrier, inc=1, device_id=(me, partner), device_id_type=MESH)

    @pl.when(has_target)
    def _():
        pl.semaphore_signal(barrier, inc=1, device_id=(me, target), device_id_type=MESH)

    @pl.when(has_source)
    def _():
        pl.semaphore_signal(barrier, inc=1, device_id=(me, source), device_id_type=MESH)

    held_fetch.start()
    first_fetch.start()
    fetch.start()

    def gradient_copy(k):
        return pltpu.make_async_remote_copy(
            src_ref=held, dst_ref=gbuf.at[me],
            send_sem=g_send.at[k - 1], recv_sem=g_recv.at[k - 1],
            device_id=(lax.rem(me + k, holders), here), device_id_type=MESH,
        )

    def own_copy(g, holder):
        return pltpu.make_async_remote_copy(
            src_ref=cbuf.at[g, holder], dst_ref=dbuf.at[g, holder],
            send_sem=c_send.at[g, holder], recv_sem=c_recv.at[g, holder],
            device_id=(me, partner), device_id_type=MESH,
        )

    def relay_copy(g, holder):
        return pltpu.make_async_remote_copy(
            src_ref=dbuf.at[g, holder], dst_ref=rbuf.at[g, holder],
            send_sem=f_send.at[g, holder], recv_sem=f_recv.at[g, holder],
            device_id=(me, target), device_id_type=MESH,
        )

    def own_tail(q, holder):
        return pltpu.make_async_remote_copy(
            src_ref=ctail.at[q, holder], dst_ref=dtail.at[q, holder],
            send_sem=ct_send.at[q, holder], recv_sem=ct_recv.at[q, holder],
            device_id=(me, partner), device_id_type=MESH,
        )

    def relay_tail(q, holder):
        return pltpu.make_async_remote_copy(
            src_ref=dtail.at[q, holder], dst_ref=rtail.at[q, holder],
            send_sem=ft_send.at[q, holder], recv_sem=ft_recv.at[q, holder],
            device_id=(me, target), device_id_type=MESH,
        )

    def convert_from(source, first, g):
        for slot in range(slots):
            for holder in range(holders):
                pieces = [
                    source[first + i, slot, owner[holder * held_levels + r]].astype(F32)
                    for i in range(PAIR) for r in range(held_levels)
                ]
                pert[g, slot, holder] = jnp.concatenate(pieces, axis=0).astype(BF16)

    def convert(g, carry=0):
        convert_from(raw, (g - 1) * PAIR, g)
        return carry

    def place_gradient(holder, block_ref):
        for slot in range(slots):
            pieces = [block_ref[slot, r] for r in range(held_levels)] * PAIR
            grad[slot, holder] = jnp.concatenate(pieces, axis=0)

    def product(g, holder, lanes):
        value = None
        for slot in range(slots):
            term = pert[g, slot, holder, :, lanes].astype(F32) * grad[slot, holder, :, lanes]
            value = term if value is None else value + term
        return value

    def control(g, holder):
        cbuf[g, holder] = product(g, holder, slice(0, main)).astype(BF16)

    held_fetch.wait()
    place_gradient(me, held)
    first_fetch.wait()
    convert_from(raw_first, 0, 0)
    control(0, me)
    pl.semaphore_wait(barrier, holders + has_target.astype(jnp.int32) + has_source.astype(jnp.int32))
    for k in range(1, holders):
        gradient_copy(k).start()
    own_copy(0, me).start()
    fetch.wait()
    for g in range(1, early):
        convert(g)
        control(g, me)
        own_copy(g, me).start()

    @pl.when(jnp.logical_not(has_source))
    def _():
        rbuf[...] = jnp.zeros_like(rbuf)
        rtail[...] = jnp.zeros_like(rtail)

    for k in range(1, holders):
        gradient_copy(k).wait_recv()
        holder = lax.rem(me + holders - k, holders)
        place_gradient(holder, gbuf.at[holder])

    for g in range(early):
        for k in range(1, holders):
            holder = lax.rem(me + k, holders)
            control(g, holder)
            own_copy(g, holder).start()

    def send_tails(q):
        for holder in range(holders):
            tails = [product(q * share + j, holder, slice(main, lon)) for j in range(share)]
            ctail[q, holder] = jnp.concatenate(tails, axis=1).astype(BF16)
            own_tail(q, holder).start()

    def pass_tails(q):
        for holder in range(holders):
            own_tail(q, holder).wait_recv()

            @pl.when(has_target)
            def _():
                relay_tail(q, holder).start()

    def send(g):
        for k in range(holders):
            holder = lax.rem(me + k, holders)
            control(g, holder)
            own_copy(g, holder).start()

    def relay_one(g, holder):
        own_copy(g, holder).wait_recv()

        @pl.when(has_target)
        def _():
            relay_copy(g, holder).start()

    def relay(g, first=0):
        for k in range(first, holders):
            relay_one(g, lax.rem(me + k, holders))

    def mix(stack):
        mixed = jnp.dot(weights[...], stack, preferred_element_type=F32)
        return mixed[:block] + mixed[block:]

    def mix_tails(q):
        @pl.when(has_source)
        def _():
            for holder in range(holders):
                relay_tail(q, holder).wait_recv()

        stack = jnp.concatenate(
            [buf[q].reshape(block, LANES) for buf in (ctail, dtail, rtail)], axis=0
        )
        mixed = mix(stack)
        for j in range(share):
            last[q * share + j] = mixed[:, j * rest:(j + 1) * rest]

    def process(g):
        @pl.when(has_source)
        def _():
            for holder in range(holders):
                relay_copy(g, holder).wait_recv()

        stack = jnp.concatenate(
            [buf[g].reshape(block, main) for buf in (cbuf, dbuf, rbuf)], axis=0
        )
        mixed = mix(stack)
        wide[:, :main] = mixed
        tail = last[g]
        wide[:, main:] = jnp.concatenate(
            [tail, mixed[:, :after], mixed[:, main - before:], tail], axis=1
        )
        for holder in range(holders):
            ring = wide[holder * inner:(holder + 1) * inner, :]
            smoothed = rho(0, 3.0) * ring
            for k in range(1, REACH + 1):
                both = pltpu.roll(ring, k, 1) + pltpu.roll(ring, width - k, 1)
                smoothed = smoothed + rho(k, 3.0) * both
            smoothed = smoothed[:, :lon]
            for slot in range(slots):
                total[slot, holder] += pert[g, slot, holder].astype(F32) * smoothed

    def stage(first, last, send_on, relay_on, process_on):
        def step(g, carry):
            if send_on:
                send(g)
            if relay_on:
                relay(g - AHEAD)
            if process_on:
                process(g - AHEAD - LAG)
            return carry

        if first < last:
            lax.fori_loop(first, last, step, 0)

    relay_one(0, me)
    convert(early)
    send(early)
    relay_one(1, me)
    convert(early + 1)
    relay(0, 1)
    send_tails(0)
    send(early + 1)
    relay(1, 1)
    total[...] = jnp.zeros_like(total)
    fill_mixing(weights, owner, holders, held_levels, rows, 1 - 2 * parity)
    lax.fori_loop(early + 2, pairs, convert, 0)
    for q in range(1, quads):
        send_tails(q)
    stage(2 * AHEAD, 2 * AHEAD + 1, True, True, False)
    pass_tails(0)
    stage(2 * AHEAD + 1, AHEAD + LAG + 1, True, True, False)
    for q in range(1, quads):
        pass_tails(q)
    mix_tails(0)
    process(0)
    stage(AHEAD + LAG + 1, pairs, True, True, True)
    for q in range(1, quads):
        mix_tails(q)
    stage(pairs, pairs + AHEAD, False, True, True)
    stage(pairs + AHEAD, pairs + AHEAD + LAG, False, False, True)

    def total_copy(k):
        return pltpu.make_async_remote_copy(
            src_ref=give.at[k - 1], dst_ref=take.at[k - 1],
            send_sem=t_send.at[k - 1], recv_sem=t_recv.at[k - 1],
            device_id=(lax.rem(me + k, holders), here), device_id_type=MESH,
        )

    for k in range(1, holders):
        holder = lax.rem(me + k, holders)
        for slot in range(slots):
            full = total[slot, holder]
            give[k - 1, slot] = sum(full[i * half:(i + 1) * half] for i in range(1, PAIR)) + full[:half]
        total_copy(k).start()

    for k in range(1, holders):
        gradient_copy(k).wait_send()

    def drain(g, carry):
        for holder in range(holders):
            own_copy(g, holder).wait_send()

            @pl.when(has_target)
            def _():
                relay_copy(g, holder).wait_send()

        return carry

    lax.fori_loop(0, pairs, drain, 0)
    for q in range(quads):
        for holder in range(holders):
            own_tail(q, holder).wait_send()

            @pl.when(has_target)
            def _():
                relay_tail(q, holder).wait_send()

    for k in range(1, holders):
        total_copy(k).wait()
    for slot in range(slots):
        full = total[slot, me]
        value = sum(full[i * half:(i + 1) * half] for i in range(1, PAIR)) + full[:half]
        for k in range(1, holders):
            value = value + take[k - 1, slot]
        for r in range(held_levels):
            out[slot, r] = value[r * rows:(r + 1) * rows]


def local(perturbations, gradient_held, block_owner):
    members, slots, levels, rows, lon = perturbations.shape
    held_levels = gradient_held.shape[1]
    holders = levels // held_levels
    pairs = members // PAIR
    inner = PAIR * held_levels * rows
    block = holders * inner
    others = max(holders - 1, 1)
    width = -(-(lon + 2 * REACH) // LANES) * LANES
    main = lon // LANES * LANES
    rest = lon - main
    share = LANES // rest
    quads = pairs // share
    part = (slots, held_levels, rows, lon)
    dma = pltpu.SemaphoreType.DMA
    return pl.pallas_call(
        kernel,
        out_shape=jax.ShapeDtypeStruct(part, F32),
        in_specs=[
            pl.BlockSpec(memory_space=pltpu.SMEM),
            pl.BlockSpec(memory_space=pltpu.HBM),
            pl.BlockSpec(memory_space=pltpu.HBM),
        ],
        out_specs=pl.BlockSpec(memory_space=pltpu.VMEM),
        scratch_shapes=[
            pltpu.VMEM((members - PAIR, slots, levels, rows, lon), BF16),
            pltpu.VMEM((PAIR, slots, levels, rows, lon), BF16),
            pltpu.VMEM(part, F32),
            pltpu.VMEM((pairs, slots, holders, inner, lon), BF16),
            pltpu.VMEM((holders,) + part, F32),
            pltpu.VMEM((slots, holders, inner, lon), F32),
            pltpu.VMEM((pairs, holders, inner, main), BF16),
            pltpu.VMEM((pairs, holders, inner, main), BF16),
            pltpu.VMEM((pairs, holders, inner, main), BF16),
            pltpu.VMEM((quads, holders, inner, LANES), BF16),
            pltpu.VMEM((quads, holders, inner, LANES), BF16),
            pltpu.VMEM((quads, holders, inner, LANES), BF16),
            pltpu.VMEM((2 * block, 3 * block), BF16),
            pltpu.VMEM((pairs, block, rest), F32),
            pltpu.VMEM((block, width), F32),
            pltpu.VMEM((slots, holders, inner, lon), F32),
            pltpu.VMEM((others, slots, held_levels * rows, lon), F32),
            pltpu.VMEM((others, slots, held_levels * rows, lon), F32),
            dma((3,)),
            dma((others,)), dma((others,)),
            dma((pairs, holders)), dma((pairs, holders)),
            dma((pairs, holders)), dma((pairs, holders)),
            dma((quads, holders)), dma((quads, holders)),
            dma((quads, holders)), dma((quads, holders)),
            dma((others,)), dma((others,)),
        ],
        compiler_params=pltpu.CompilerParams(
            collective_id=0, has_side_effects=True, vmem_limit_bytes=538 * 1024 * 1024 // 10
        ),
    )(block_owner, perturbations, gradient_held)


def solution(mesh):
    placed = (P("mem", None, None, "lat", None), P(None, "mem", "lat", None), P())
    return jax.shard_map(
        local, mesh=mesh, in_specs=placed, out_specs=P(None, "mem", "lat", None), check_vma=False,
    )
```

```python
import functools
import math

import jax
import jax.numpy as jnp
from jax import lax
from jax.experimental import pallas as pl
from jax.experimental.pallas import tpu as pltpu
from jax.sharding import PartitionSpec as P

MESH = pl.DeviceIdType.MESH
REACH = 4
LANES = 128
PAIR = 2
AHEAD = 2
LAG = 4
F32 = jnp.float32
BF16 = jnp.bfloat16


def rho(offset, spread):
    return math.exp(-(offset * offset) / (2.0 * spread * spread))


def rho_of(apart, spread):
    value = jnp.zeros(apart.shape, F32)
    for a in range(REACH + 1):
        value = jnp.where(jnp.abs(apart) == a, rho(a, spread), value)
    return value


def fill_mixing(weights, owner, holders, held_levels, rows, direct):
    inner = PAIR * held_levels * rows
    block = holders * inner

    def places(axis):
        index = lax.broadcasted_iota(jnp.int32, (block, 3 * block), axis)
        part = jnp.where(index >= block, 1, 0) + jnp.where(index >= 2 * block, 1, 0)
        index = index - part * block
        level = jnp.zeros_like(index)
        member = jnp.zeros_like(index)
        row = index
        for p in range(holders * held_levels):
            for i in range(PAIR):
                start = (p // held_levels) * inner + (i * held_levels + p % held_levels) * rows
                inside = jnp.logical_and(index >= start, index < start + rows)
                level = jnp.where(inside, owner[p], level)
                member = jnp.where(inside, i, member)
                row = jnp.where(inside, index - start, row)
        shift = jnp.where(part == 1, direct, jnp.where(part == 2, -direct, 0))
        return level, member, row + shift * rows

    to_level, to_member, to_row = places(0)
    from_level, from_member, from_row = places(1)
    exact = rho_of(from_level - to_level, 2.0) * rho_of(from_row - to_row, 2.5)
    exact = jnp.where(from_member == to_member, exact, 0.0)
    high = exact.astype(BF16)
    weights[:block, :] = high
    weights[block:, :] = (exact - high.astype(F32)).astype(BF16)


def kernel(
    owner, fields, held_far, out,
    raw, raw_first, held, pert, gbuf, grad, cbuf, dbuf, rbuf, ctail, dtail, rtail, weights, last, wide, total, give, take,
    p_sem, g_send, g_recv, c_send, c_recv, f_send, f_recv,
    ct_send, ct_recv, ft_send, ft_recv, t_send, t_recv,
):
    members, slots, levels, rows, lon = fields.shape
    held_levels = held.shape[1]
    holders = levels // held_levels
    pairs = members // PAIR
    inner = PAIR * held_levels * rows
    block = holders * inner
    half = held_levels * rows
    width = wide.shape[1]
    main = cbuf.shape[-1]
    rest = lon - main
    share = LANES // rest
    quads = pairs // share
    after = (width - lon) // 2
    before = width - lon - after - rest
    early = min(AHEAD, pairs)

    first_fetch = pltpu.make_async_copy(fields.at[pl.ds(0, PAIR)], raw_first, p_sem.at[0])
    held_fetch = pltpu.make_async_copy(held_far, held, p_sem.at[1])
    fetch = pltpu.make_async_copy(fields.at[pl.ds(PAIR, members - PAIR)], raw, p_sem.at[2])

    me = lax.axis_index("mem")
    here = lax.axis_index("lat")
    count = lax.axis_size("lat")
    parity = lax.rem(here, 2)
    partner = here + 1 - 2 * parity
    hop = 2 - 4 * parity
    target = here + hop
    source = here - hop
    has_target = jnp.logical_and(target >= 0, target < count)
    has_source = jnp.logical_and(source >= 0, source < count)

    barrier = pltpu.get_barrier_semaphore()
    for k in range(1, holders):
        pl.semaphore_signal(
            barrier, inc=1, device_id=(lax.rem(me + k, holders), here), device_id_type=MESH
        )
    pl.semaphore_signal(barrier, inc=1, device_id=(me, partner), device_id_type=MESH)

    @pl.when(has_target)
    def _():
        pl.semaphore_signal(barrier, inc=1, device_id=(me, target), device_id_type=MESH)

    @pl.when(has_source)
    def _():
        pl.semaphore_signal(barrier, inc=1, device_id=(me, source), device_id_type=MESH)

    held_fetch.start()
    first_fetch.start()
    fetch.start()

    def gradient_copy(k):
        return pltpu.make_async_remote_copy(
            src_ref=held, dst_ref=gbuf.at[me],
            send_sem=g_send.at[k - 1], recv_sem=g_recv.at[k - 1],
            device_id=(lax.rem(me + k, holders), here), device_id_type=MESH,
        )

    def own_copy(g, holder):
        return pltpu.make_async_remote_copy(
            src_ref=cbuf.at[g, holder], dst_ref=dbuf.at[g, holder],
            send_sem=c_send.at[g, holder], recv_sem=c_recv.at[g, holder],
            device_id=(me, partner), device_id_type=MESH,
        )

    def relay_copy(g, holder):
        return pltpu.make_async_remote_copy(
            src_ref=dbuf.at[g, holder], dst_ref=rbuf.at[g, holder],
            send_sem=f_send.at[g, holder], recv_sem=f_recv.at[g, holder],
            device_id=(me, target), device_id_type=MESH,
        )

    def own_tail(q, holder):
        return pltpu.make_async_remote_copy(
            src_ref=ctail.at[q, holder], dst_ref=dtail.at[q, holder],
            send_sem=ct_send.at[q, holder], recv_sem=ct_recv.at[q, holder],
            device_id=(me, partner), device_id_type=MESH,
        )

    def relay_tail(q, holder):
        return pltpu.make_async_remote_copy(
            src_ref=dtail.at[q, holder], dst_ref=rtail.at[q, holder],
            send_sem=ft_send.at[q, holder], recv_sem=ft_recv.at[q, holder],
            device_id=(me, target), device_id_type=MESH,
        )

    def convert_from(source, first, g):
        for slot in range(slots):
            for holder in range(holders):
                pieces = [
                    source[first + i, slot, owner[holder * held_levels + r]].astype(F32)
                    for i in range(PAIR) for r in range(held_levels)
                ]
                pert[g, slot, holder] = jnp.concatenate(pieces, axis=0).astype(BF16)

    def convert(g, carry=0):
        convert_from(raw, (g - 1) * PAIR, g)
        return carry

    def place_gradient(holder, block_ref):
        for slot in range(slots):
            pieces = [block_ref[slot, r] for r in range(held_levels)] * PAIR
            grad[slot, holder] = jnp.concatenate(pieces, axis=0)

    def product(g, holder, lanes):
        value = None
        for slot in range(slots):
            term = pert[g, slot, holder, :, lanes].astype(F32) * grad[slot, holder, :, lanes]
            value = term if value is None else value + term
        return value

    def control(g, holder):
        cbuf[g, holder] = product(g, holder, slice(0, main)).astype(BF16)

    held_fetch.wait()
    place_gradient(me, held)
    first_fetch.wait()
    convert_from(raw_first, 0, 0)
    control(0, me)
    pl.semaphore_wait(barrier, holders + has_target.astype(jnp.int32) + has_source.astype(jnp.int32))
    for k in range(1, holders):
        gradient_copy(k).start()
    own_copy(0, me).start()
    fetch.wait()
    for g in range(1, early):
        convert(g)
        control(g, me)
        own_copy(g, me).start()

    @pl.when(jnp.logical_not(has_source))
    def _():
        rbuf[...] = jnp.zeros_like(rbuf)
        rtail[...] = jnp.zeros_like(rtail)

    for k in range(1, holders):
        gradient_copy(k).wait_recv()
        holder = lax.rem(me + holders - k, holders)
        place_gradient(holder, gbuf.at[holder])

    for g in range(early):
        for k in range(1, holders):
            holder = lax.rem(me + k, holders)
            control(g, holder)
            own_copy(g, holder).start()

    def send_tails(q):
        for holder in range(holders):
            tails = [product(q * share + j, holder, slice(main, lon)) for j in range(share)]
            ctail[q, holder] = jnp.concatenate(tails, axis=1).astype(BF16)
            own_tail(q, holder).start()

    def pass_tails(q):
        for holder in range(holders):
            own_tail(q, holder).wait_recv()

            @pl.when(has_target)
            def _():
                relay_tail(q, holder).start()

    def send(g):
        for k in range(holders):
            holder = lax.rem(me + k, holders)
            control(g, holder)
            own_copy(g, holder).start()

    def relay_one(g, holder):
        own_copy(g, holder).wait_recv()

        @pl.when(has_target)
        def _():
            relay_copy(g, holder).start()

    def relay(g, first=0):
        for k in range(first, holders):
            relay_one(g, lax.rem(me + k, holders))

    def mix(stack):
        mixed = jnp.dot(weights[...], stack, preferred_element_type=F32)
        return mixed[:block] + mixed[block:]

    def mix_tails(q):
        @pl.when(has_source)
        def _():
            for holder in range(holders):
                relay_tail(q, holder).wait_recv()

        stack = jnp.concatenate(
            [buf[q].reshape(block, LANES) for buf in (ctail, dtail, rtail)], axis=0
        )
        mixed = mix(stack)
        for j in range(share):
            last[q * share + j] = mixed[:, j * rest:(j + 1) * rest]

    def process(g):
        @pl.when(has_source)
        def _():
            for holder in range(holders):
                relay_copy(g, holder).wait_recv()

        stack = jnp.concatenate(
            [buf[g].reshape(block, main) for buf in (cbuf, dbuf, rbuf)], axis=0
        )
        mixed = mix(stack)
        wide[:, :main] = mixed
        tail = last[g]
        wide[:, main:] = jnp.concatenate(
            [tail, mixed[:, :after], mixed[:, main - before:], tail], axis=1
        )
        for holder in range(holders):
            ring = wide[holder * inner:(holder + 1) * inner, :]
            smoothed = rho(0, 3.0) * ring
            for k in range(1, REACH + 1):
                both = pltpu.roll(ring, k, 1) + pltpu.roll(ring, width - k, 1)
                smoothed = smoothed + rho(k, 3.0) * both
            smoothed = smoothed[:, :lon]
            for slot in range(slots):
                total[slot, holder] += pert[g, slot, holder].astype(F32) * smoothed

    def stage(first, last, send_on, relay_on, process_on):
        def step(g, carry):
            if relay_on:
                relay_one(g - AHEAD, me)
            if send_on:
                send(g)
            if relay_on:
                relay(g - AHEAD, 1)
            if process_on:
                process(g - AHEAD - LAG)
            return carry

        if first < last:
            lax.fori_loop(first, last, step, 0)

    relay_one(0, me)
    convert(early)
    send(early)
    relay_one(1, me)
    convert(early + 1)
    relay(0, 1)
    send_tails(0)
    send(early + 1)
    relay(1, 1)
    total[...] = jnp.zeros_like(total)
    fill_mixing(weights, owner, holders, held_levels, rows, 1 - 2 * parity)
    lax.fori_loop(early + 2, pairs, convert, 0)
    for q in range(1, quads):
        send_tails(q)
    stage(2 * AHEAD, 2 * AHEAD + 1, True, True, False)
    pass_tails(0)
    stage(2 * AHEAD + 1, AHEAD + LAG + 1, True, True, False)
    for q in range(1, quads):
        pass_tails(q)
    mix_tails(0)
    process(0)
    stage(AHEAD + LAG + 1, pairs, True, True, True)
    for q in range(1, quads):
        mix_tails(q)
    stage(pairs, pairs + AHEAD, False, True, True)
    stage(pairs + AHEAD, pairs + AHEAD + LAG, False, False, True)

    def total_copy(k):
        return pltpu.make_async_remote_copy(
            src_ref=give.at[k - 1], dst_ref=take.at[k - 1],
            send_sem=t_send.at[k - 1], recv_sem=t_recv.at[k - 1],
            device_id=(lax.rem(me + k, holders), here), device_id_type=MESH,
        )

    for k in range(1, holders):
        holder = lax.rem(me + k, holders)
        for slot in range(slots):
            full = total[slot, holder]
            give[k - 1, slot] = sum(full[i * half:(i + 1) * half] for i in range(1, PAIR)) + full[:half]
        total_copy(k).start()

    for k in range(1, holders):
        gradient_copy(k).wait_send()

    def drain(g, carry):
        for holder in range(holders):
            own_copy(g, holder).wait_send()

            @pl.when(has_target)
            def _():
                relay_copy(g, holder).wait_send()

        return carry

    lax.fori_loop(0, pairs, drain, 0)
    for q in range(quads):
        for holder in range(holders):
            own_tail(q, holder).wait_send()

            @pl.when(has_target)
            def _():
                relay_tail(q, holder).wait_send()

    for k in range(1, holders):
        total_copy(k).wait()
    for slot in range(slots):
        full = total[slot, me]
        value = sum(full[i * half:(i + 1) * half] for i in range(1, PAIR)) + full[:half]
        for k in range(1, holders):
            value = value + take[k - 1, slot]
        for r in range(held_levels):
            out[slot, r] = value[r * rows:(r + 1) * rows]


def local(perturbations, gradient_held, block_owner):
    members, slots, levels, rows, lon = perturbations.shape
    held_levels = gradient_held.shape[1]
    holders = levels // held_levels
    pairs = members // PAIR
    inner = PAIR * held_levels * rows
    block = holders * inner
    others = max(holders - 1, 1)
    width = -(-(lon + 2 * REACH) // LANES) * LANES
    main = lon // LANES * LANES
    rest = lon - main
    share = LANES // rest
    quads = pairs // share
    part = (slots, held_levels, rows, lon)
    dma = pltpu.SemaphoreType.DMA
    return pl.pallas_call(
        kernel,
        out_shape=jax.ShapeDtypeStruct(part, F32),
        in_specs=[
            pl.BlockSpec(memory_space=pltpu.SMEM),
            pl.BlockSpec(memory_space=pltpu.HBM),
            pl.BlockSpec(memory_space=pltpu.HBM),
        ],
        out_specs=pl.BlockSpec(memory_space=pltpu.VMEM),
        scratch_shapes=[
            pltpu.VMEM((members - PAIR, slots, levels, rows, lon), BF16),
            pltpu.VMEM((PAIR, slots, levels, rows, lon), BF16),
            pltpu.VMEM(part, F32),
            pltpu.VMEM((pairs, slots, holders, inner, lon), BF16),
            pltpu.VMEM((holders,) + part, F32),
            pltpu.VMEM((slots, holders, inner, lon), F32),
            pltpu.VMEM((pairs, holders, inner, main), BF16),
            pltpu.VMEM((pairs, holders, inner, main), BF16),
            pltpu.VMEM((pairs, holders, inner, main), BF16),
            pltpu.VMEM((quads, holders, inner, LANES), BF16),
            pltpu.VMEM((quads, holders, inner, LANES), BF16),
            pltpu.VMEM((quads, holders, inner, LANES), BF16),
            pltpu.VMEM((2 * block, 3 * block), BF16),
            pltpu.VMEM((pairs, block, rest), F32),
            pltpu.VMEM((block, width), F32),
            pltpu.VMEM((slots, holders, inner, lon), F32),
            pltpu.VMEM((others, slots, held_levels * rows, lon), F32),
            pltpu.VMEM((others, slots, held_levels * rows, lon), F32),
            dma((3,)),
            dma((others,)), dma((others,)),
            dma((pairs, holders)), dma((pairs, holders)),
            dma((pairs, holders)), dma((pairs, holders)),
            dma((quads, holders)), dma((quads, holders)),
            dma((quads, holders)), dma((quads, holders)),
            dma((others,)), dma((others,)),
        ],
        compiler_params=pltpu.CompilerParams(
            collective_id=0, has_side_effects=True, vmem_limit_bytes=538 * 1024 * 1024 // 10
        ),
    )(block_owner, perturbations, gradient_held)


def solution(mesh):
    placed = (P("mem", None, None, "lat", None), P(None, "mem", "lat", None), P())
    return jax.shard_map(
        local, mesh=mesh, in_specs=placed, out_specs=P(None, "mem", "lat", None), check_vma=False,
    )
```

```python
import functools
import math

import jax
import jax.numpy as jnp
from jax import lax
from jax.experimental import pallas as pl
from jax.experimental.pallas import tpu as pltpu
from jax.sharding import PartitionSpec as P

MESH = pl.DeviceIdType.MESH
REACH = 4
LANES = 128
PAIR = 2
AHEAD = 2
LAG = 3
F32 = jnp.float32
BF16 = jnp.bfloat16


def rho(offset, spread):
    return math.exp(-(offset * offset) / (2.0 * spread * spread))


def rho_of(apart, spread):
    value = jnp.zeros(apart.shape, F32)
    for a in range(REACH + 1):
        value = jnp.where(jnp.abs(apart) == a, rho(a, spread), value)
    return value


def fill_mixing(weights, owner, holders, held_levels, rows, direct):
    inner = PAIR * held_levels * rows
    block = holders * inner

    def places(axis):
        index = lax.broadcasted_iota(jnp.int32, (block, 3 * block), axis)
        part = jnp.where(index >= block, 1, 0) + jnp.where(index >= 2 * block, 1, 0)
        index = index - part * block
        level = jnp.zeros_like(index)
        member = jnp.zeros_like(index)
        row = index
        for p in range(holders * held_levels):
            for i in range(PAIR):
                start = (p // held_levels) * inner + (i * held_levels + p % held_levels) * rows
                inside = jnp.logical_and(index >= start, index < start + rows)
                level = jnp.where(inside, owner[p], level)
                member = jnp.where(inside, i, member)
                row = jnp.where(inside, index - start, row)
        shift = jnp.where(part == 1, direct, jnp.where(part == 2, -direct, 0))
        return level, member, row + shift * rows

    to_level, to_member, to_row = places(0)
    from_level, from_member, from_row = places(1)
    exact = rho_of(from_level - to_level, 2.0) * rho_of(from_row - to_row, 2.5)
    exact = jnp.where(from_member == to_member, exact, 0.0)
    high = exact.astype(BF16)
    weights[:block, :] = high
    weights[block:, :] = (exact - high.astype(F32)).astype(BF16)


def kernel(
    owner, fields, held_far, out,
    raw, raw_first, held, pert, gbuf, grad, cbuf, dbuf, rbuf, ctail, dtail, rtail, weights, last, wide, total, give, take,
    p_sem, g_send, g_recv, c_send, c_recv, f_send, f_recv,
    ct_send, ct_recv, ft_send, ft_recv, t_send, t_recv,
):
    members, slots, levels, rows, lon = fields.shape
    held_levels = held.shape[1]
    holders = levels // held_levels
    pairs = members // PAIR
    inner = PAIR * held_levels * rows
    block = holders * inner
    half = held_levels * rows
    width = wide.shape[1]
    main = cbuf.shape[-1]
    rest = lon - main
    share = LANES // rest
    quads = pairs // share
    after = (width - lon) // 2
    before = width - lon - after - rest
    early = min(AHEAD, pairs)

    first_fetch = pltpu.make_async_copy(fields.at[pl.ds(0, PAIR)], raw_first, p_sem.at[0])
    held_fetch = pltpu.make_async_copy(held_far, held, p_sem.at[1])
    fetch = pltpu.make_async_copy(fields.at[pl.ds(PAIR, members - PAIR)], raw, p_sem.at[2])

    me = lax.axis_index("mem")
    here = lax.axis_index("lat")
    count = lax.axis_size("lat")
    parity = lax.rem(here, 2)
    partner = here + 1 - 2 * parity
    hop = 2 - 4 * parity
    target = here + hop
    source = here - hop
    has_target = jnp.logical_and(target >= 0, target < count)
    has_source = jnp.logical_and(source >= 0, source < count)

    barrier = pltpu.get_barrier_semaphore()
    for k in range(1, holders):
        pl.semaphore_signal(
            barrier, inc=1, device_id=(lax.rem(me + k, holders), here), device_id_type=MESH
        )
    pl.semaphore_signal(barrier, inc=1, device_id=(me, partner), device_id_type=MESH)

    @pl.when(has_target)
    def _():
        pl.semaphore_signal(barrier, inc=1, device_id=(me, target), device_id_type=MESH)

    @pl.when(has_source)
    def _():
        pl.semaphore_signal(barrier, inc=1, device_id=(me, source), device_id_type=MESH)

    held_fetch.start()
    first_fetch.start()
    fetch.start()

    def gradient_copy(k):
        return pltpu.make_async_remote_copy(
            src_ref=held, dst_ref=gbuf.at[me],
            send_sem=g_send.at[k - 1], recv_sem=g_recv.at[k - 1],
            device_id=(lax.rem(me + k, holders), here), device_id_type=MESH,
        )

    def own_copy(g, holder):
        return pltpu.make_async_remote_copy(
            src_ref=cbuf.at[g, holder], dst_ref=dbuf.at[g, holder],
            send_sem=c_send.at[g, holder], recv_sem=c_recv.at[g, holder],
            device_id=(me, partner), device_id_type=MESH,
        )

    def relay_copy(g, holder):
        return pltpu.make_async_remote_copy(
            src_ref=dbuf.at[g, holder], dst_ref=rbuf.at[g, holder],
            send_sem=f_send.at[g, holder], recv_sem=f_recv.at[g, holder],
            device_id=(me, target), device_id_type=MESH,
        )

    def own_tail(q, holder):
        return pltpu.make_async_remote_copy(
            src_ref=ctail.at[q, holder], dst_ref=dtail.at[q, holder],
            send_sem=ct_send.at[q, holder], recv_sem=ct_recv.at[q, holder],
            device_id=(me, partner), device_id_type=MESH,
        )

    def relay_tail(q, holder):
        return pltpu.make_async_remote_copy(
            src_ref=dtail.at[q, holder], dst_ref=rtail.at[q, holder],
            send_sem=ft_send.at[q, holder], recv_sem=ft_recv.at[q, holder],
            device_id=(me, target), device_id_type=MESH,
        )

    def convert_from(source, first, g):
        for slot in range(slots):
            for holder in range(holders):
                pieces = [
                    source[first + i, slot, owner[holder * held_levels + r]].astype(F32)
                    for i in range(PAIR) for r in range(held_levels)
                ]
                pert[g, slot, holder] = jnp.concatenate(pieces, axis=0).astype(BF16)

    def convert(g, carry=0):
        convert_from(raw, (g - 1) * PAIR, g)
        return carry

    def place_gradient(holder, block_ref):
        for slot in range(slots):
            pieces = [block_ref[slot, r] for r in range(held_levels)] * PAIR
            grad[slot, holder] = jnp.concatenate(pieces, axis=0)

    def product(g, holder, lanes):
        value = None
        for slot in range(slots):
            term = pert[g, slot, holder, :, lanes].astype(F32) * grad[slot, holder, :, lanes]
            value = term if value is None else value + term
        return value

    def control(g, holder):
        cbuf[g, holder] = product(g, holder, slice(0, main)).astype(BF16)

    held_fetch.wait()
    place_gradient(me, held)
    first_fetch.wait()
    convert_from(raw_first, 0, 0)
    control(0, me)
    pl.semaphore_wait(barrier, holders + has_target.astype(jnp.int32) + has_source.astype(jnp.int32))
    for k in range(1, holders):
        gradient_copy(k).start()
    own_copy(0, me).start()
    fetch.wait()
    for g in range(1, early):
        convert(g)
        control(g, me)
        own_copy(g, me).start()

    @pl.when(jnp.logical_not(has_source))
    def _():
        rbuf[...] = jnp.zeros_like(rbuf)
        rtail[...] = jnp.zeros_like(rtail)

    for k in range(1, holders):
        gradient_copy(k).wait_recv()
        holder = lax.rem(me + holders - k, holders)
        place_gradient(holder, gbuf.at[holder])

    for g in range(early):
        for k in range(1, holders):
            holder = lax.rem(me + k, holders)
            control(g, holder)
            own_copy(g, holder).start()

    def send_tails(q):
        for holder in range(holders):
            tails = [product(q * share + j, holder, slice(main, lon)) for j in range(share)]
            ctail[q, holder] = jnp.concatenate(tails, axis=1).astype(BF16)
            own_tail(q, holder).start()

    def pass_tails(q):
        for holder in range(holders):
            own_tail(q, holder).wait_recv()

            @pl.when(has_target)
            def _():
                relay_tail(q, holder).start()

    def send(g):
        for k in range(holders):
            holder = lax.rem(me + k, holders)
            control(g, holder)
            own_copy(g, holder).start()

    def relay_one(g, holder):
        own_copy(g, holder).wait_recv()

        @pl.when(has_target)
        def _():
            relay_copy(g, holder).start()

    def relay(g, first=0):
        for k in range(first, holders):
            relay_one(g, lax.rem(me + k, holders))

    def mix(stack):
        mixed = jnp.dot(weights[...], stack, preferred_element_type=F32)
        return mixed[:block] + mixed[block:]

    def mix_tails(q):
        @pl.when(has_source)
        def _():
            for holder in range(holders):
                relay_tail(q, holder).wait_recv()

        stack = jnp.concatenate(
            [buf[q].reshape(block, LANES) for buf in (ctail, dtail, rtail)], axis=0
        )
        mixed = mix(stack)
        for j in range(share):
            last[q * share + j] = mixed[:, j * rest:(j + 1) * rest]

    def process(g):
        @pl.when(has_source)
        def _():
            for holder in range(holders):
                relay_copy(g, holder).wait_recv()

        stack = jnp.concatenate(
            [buf[g].reshape(block, main) for buf in (cbuf, dbuf, rbuf)], axis=0
        )
        mixed = mix(stack)
        wide[:, :main] = mixed
        tail = last[g]
        wide[:, main:] = jnp.concatenate(
            [tail, mixed[:, :after], mixed[:, main - before:], tail], axis=1
        )
        for holder in range(holders):
            ring = wide[holder * inner:(holder + 1) * inner, :]
            smoothed = rho(0, 3.0) * ring
            for k in range(1, REACH + 1):
                both = pltpu.roll(ring, k, 1) + pltpu.roll(ring, width - k, 1)
                smoothed = smoothed + rho(k, 3.0) * both
            smoothed = smoothed[:, :lon]
            for slot in range(slots):
                total[slot, holder] += pert[g, slot, holder].astype(F32) * smoothed

    def stage(first, last, send_on, relay_on, process_on):
        def step(g, carry):
            if relay_on:
                relay_one(g - AHEAD, me)
            if send_on:
                send(g)
            if relay_on:
                relay(g - AHEAD, 1)
            if process_on:
                process(g - AHEAD - LAG)
            return carry

        if first < last:
            lax.fori_loop(first, last, step, 0)

    relay_one(0, me)
    convert(early)
    send(early)
    relay_one(1, me)
    convert(early + 1)
    relay(0, 1)
    send_tails(0)
    send(early + 1)
    relay(1, 1)
    total[...] = jnp.zeros_like(total)
    fill_mixing(weights, owner, holders, held_levels, rows, 1 - 2 * parity)
    lax.fori_loop(early + 2, pairs, convert, 0)
    for q in range(1, quads):
        send_tails(q)
    stage(2 * AHEAD, 2 * AHEAD + 1, True, True, False)
    pass_tails(0)
    stage(2 * AHEAD + 1, AHEAD + LAG + 1, True, True, False)
    for q in range(1, quads):
        pass_tails(q)
    mix_tails(0)
    process(0)
    stage(AHEAD + LAG + 1, pairs, True, True, True)
    for q in range(1, quads):
        mix_tails(q)
    stage(pairs, pairs + AHEAD, False, True, True)
    stage(pairs + AHEAD, pairs + AHEAD + LAG, False, False, True)

    def total_copy(k):
        return pltpu.make_async_remote_copy(
            src_ref=give.at[k - 1], dst_ref=take.at[k - 1],
            send_sem=t_send.at[k - 1], recv_sem=t_recv.at[k - 1],
            device_id=(lax.rem(me + k, holders), here), device_id_type=MESH,
        )

    for k in range(1, holders):
        holder = lax.rem(me + k, holders)
        for slot in range(slots):
            full = total[slot, holder]
            give[k - 1, slot] = sum(full[i * half:(i + 1) * half] for i in range(1, PAIR)) + full[:half]
        total_copy(k).start()

    for k in range(1, holders):
        gradient_copy(k).wait_send()

    def drain(g, carry):
        for holder in range(holders):
            own_copy(g, holder).wait_send()

            @pl.when(has_target)
            def _():
                relay_copy(g, holder).wait_send()

        return carry

    lax.fori_loop(0, pairs, drain, 0)
    for q in range(quads):
        for holder in range(holders):
            own_tail(q, holder).wait_send()

            @pl.when(has_target)
            def _():
                relay_tail(q, holder).wait_send()

    for k in range(1, holders):
        total_copy(k).wait()
    for slot in range(slots):
        full = total[slot, me]
        value = sum(full[i * half:(i + 1) * half] for i in range(1, PAIR)) + full[:half]
        for k in range(1, holders):
            value = value + take[k - 1, slot]
        for r in range(held_levels):
            out[slot, r] = value[r * rows:(r + 1) * rows]


def local(perturbations, gradient_held, block_owner):
    members, slots, levels, rows, lon = perturbations.shape
    held_levels = gradient_held.shape[1]
    holders = levels // held_levels
    pairs = members // PAIR
    inner = PAIR * held_levels * rows
    block = holders * inner
    others = max(holders - 1, 1)
    width = -(-(lon + 2 * REACH) // LANES) * LANES
    main = lon // LANES * LANES
    rest = lon - main
    share = LANES // rest
    quads = pairs // share
    part = (slots, held_levels, rows, lon)
    dma = pltpu.SemaphoreType.DMA
    return pl.pallas_call(
        kernel,
        out_shape=jax.ShapeDtypeStruct(part, F32),
        in_specs=[
            pl.BlockSpec(memory_space=pltpu.SMEM),
            pl.BlockSpec(memory_space=pltpu.HBM),
            pl.BlockSpec(memory_space=pltpu.HBM),
        ],
        out_specs=pl.BlockSpec(memory_space=pltpu.VMEM),
        scratch_shapes=[
            pltpu.VMEM((members - PAIR, slots, levels, rows, lon), BF16),
            pltpu.VMEM((PAIR, slots, levels, rows, lon), BF16),
            pltpu.VMEM(part, F32),
            pltpu.VMEM((pairs, slots, holders, inner, lon), BF16),
            pltpu.VMEM((holders,) + part, F32),
            pltpu.VMEM((slots, holders, inner, lon), F32),
            pltpu.VMEM((pairs, holders, inner, main), BF16),
            pltpu.VMEM((pairs, holders, inner, main), BF16),
            pltpu.VMEM((pairs, holders, inner, main), BF16),
            pltpu.VMEM((quads, holders, inner, LANES), BF16),
            pltpu.VMEM((quads, holders, inner, LANES), BF16),
            pltpu.VMEM((quads, holders, inner, LANES), BF16),
            pltpu.VMEM((2 * block, 3 * block), BF16),
            pltpu.VMEM((pairs, block, rest), F32),
            pltpu.VMEM((block, width), F32),
            pltpu.VMEM((slots, holders, inner, lon), F32),
            pltpu.VMEM((others, slots, held_levels * rows, lon), F32),
            pltpu.VMEM((others, slots, held_levels * rows, lon), F32),
            dma((3,)),
            dma((others,)), dma((others,)),
            dma((pairs, holders)), dma((pairs, holders)),
            dma((pairs, holders)), dma((pairs, holders)),
            dma((quads, holders)), dma((quads, holders)),
            dma((quads, holders)), dma((quads, holders)),
            dma((others,)), dma((others,)),
        ],
        compiler_params=pltpu.CompilerParams(
            collective_id=0, has_side_effects=True, vmem_limit_bytes=538 * 1024 * 1024 // 10
        ),
    )(block_owner, perturbations, gradient_held)


def solution(mesh):
    placed = (P("mem", None, None, "lat", None), P(None, "mem", "lat", None), P())
    return jax.shard_map(
        local, mesh=mesh, in_specs=placed, out_specs=P(None, "mem", "lat", None), check_vma=False,
    )
```
